32 devices in a mesh: seq: 8 (over z, x), head: 4 (over y, core).
Axes of the slice: x: 2, y: 2, z: 4, core: 2. Of those that a mesh axis runs over, the one named last changes fastest.
Arguments:
- queries: bfloat16 [2048, 1024], P('seq', 'head'), may hold values from -40 to 40
- keys: bfloat16 [2048, 1024], P('seq', 'head'), may hold values from -12 to 12
- values: bfloat16 [2048, 1024], P('seq', 'head'), may hold values from -6 to 6
- residual: bfloat16 [2048, 1024], P('seq', 'head'), may hold values from -3 to 3
- reg_weight: bfloat16 [1024, 1024], P('head'), may hold values from -0.1875 to 0.1875
- targets: bfloat16 [32, 16, 1024], P('seq'), may hold values from -3 to 3
- block_track: int32 [16], replicated, may hold values from 0 to 31
- row_count: int32 [16], P('seq'), may hold values from 1 to 128, 1536 in all
- pool_slot: int32 [16, 128], P('seq'), may hold values from 0 to 15
Outputs:
- grad_reg: bfloat16 [1024, 1024], P('head')
- context_grad: bfloat16 [2048, 1024], P('seq', 'head')
The draws below stay inside these ranges and needn't reach their ends.
All inputs are finite; a program needn't handle non-finite values. No bound on the sum of `row_count` on one device may be relied on, other than what follows from the above.
Results may differ from the reference program's by a relative error of at most 0.019.
Values may be sent and summed in bfloat16 or wider, within the bound.
A program may use at most 128 MiB of HBM per device.

```python
import math
import jax
import jax.numpy as jnp
import numpy as np
from jax import lax

D = 1024
HEADS = 16
HEAD_DIM = 64
TARGET_D = 1024
BLK = 128
POOL = 16
TOKENS = 2048
BLOCKS = 16
TRACKS = 32


def shared_attention(key):
    base = jax.random.fold_in(key, 101)
    query_key, key_key = jax.random.split(base, 2)
    query_draw = jnp.clip(1.6 * jax.random.normal(query_key, (TOKENS, D), jnp.float32), -11.0, 11.0)
    key_draw = jnp.clip(1.6 * jax.random.normal(key_key, (TOKENS, D), jnp.float32), -11.0, 11.0)
    return (query_draw, key_draw)


def draw_queries(key, part):
    return shared_attention(key)[0].astype(jnp.bfloat16)


def draw_keys(key, part):
    return shared_attention(key)[1].astype(jnp.bfloat16)


def plant(drawn, stream_key, smallest, top_value):
    spot = [jax.random.randint(jax.random.fold_in(stream_key, axis), (), 0, length) for axis, length in enumerate(drawn.shape)]
    widest = drawn.shape.index(max(drawn.shape))
    neighbour = spot[:widest] + [(spot[widest] + 1) % drawn.shape[widest]] + spot[widest + 1:]
    return drawn.at[tuple(spot)].set(smallest).at[tuple(neighbour)].set(top_value)


def shard_levels(key, shape, cuts, smallest, high):
    loudness, own = 1.0, jax.random.fold_in(key, 6)
    for dim, shards_of in cuts:
        steps = jnp.exp(jax.random.uniform(jax.random.fold_in(own, dim), (shards_of,), jnp.float32, smallest / len(cuts), high / len(cuts)))
        loudness = loudness * jnp.repeat(steps, shape[dim] // shards_of).reshape([-1 if axis == dim else 1 for axis in range(len(shape))])
    return loudness


def cumulative_ranks(count, skew):
    loads = [(1 << 20) // math.isqrt(standing ** skew) + 1 for standing in range(1, count + 1)]
    scale = 1 + sum(loads) // (1 << 30)
    return np.cumsum(np.array([max(1, weight // scale) for weight in loads]))


def skewed_ids(own_key, dims, amount, lean):
    listing = cumulative_ranks(amount, lean)
    lot = jax.random.randint(jax.random.fold_in(own_key, 1), dims, 0, int(listing[amount - 1]))
    standing = jnp.searchsorted(jnp.asarray(listing, jnp.int32), lot, side="right")
    return jax.random.permutation(jax.random.fold_in(own_key, 2), amount)[standing].astype(jnp.int32)


def split_up(count, total, limit, skew):
    portions = [(1 << 20) // math.isqrt(standing ** skew) + 1 for standing in range(2, count + 1)]
    rest, holding = total - limit - (count - 1), [1] * (count - 1)
    while rest > 0:
        free = [i for i in range(count - 1) if holding[i] < limit]
        mass, budget = sum([portions[i] for i in free]), rest
        for i in free:
            addition = min(limit - holding[i], max(1, budget * portions[i] // mass), rest)
            holding[i] = holding[i] + addition
            rest = rest - addition
    return np.array([limit] + holding)


def ragged_sizes(own_key, amount, total, limit, slope):
    if amount == 2:
        one = jax.random.randint(own_key, (), max(1, total - limit), min(limit, total - 1) + 1)
        return jnp.stack([one, total - one])
    lengths = jnp.asarray(split_up(amount, total, limit, slope), jnp.int32)
    pairs = (amount - 1) // 2
    source_of, taker = lengths[1:1 + 2 * pairs:2], lengths[2:2 + 2 * pairs:2]
    slack = jnp.minimum(source_of - 1, limit - taker)
    passed = jax.random.randint(jax.random.fold_in(own_key, 1), (pairs,), 0, 1 << 20) % (slack + 1)
    lengths = lengths.at[1:1 + 2 * pairs:2].set(source_of - passed).at[2:2 + 2 * pairs:2].set(taker + passed)
    return lengths[jax.random.permutation(jax.random.fold_in(own_key, 2), amount)]


def centred(key, extent, spread, reach, cuts=(), kind=jnp.bfloat16):
    drawn = spread * jax.random.normal(key, extent, jnp.float32)
    if cuts:
        drawn = drawn * shard_levels(key, extent, cuts, -0.22, 0.18)
    return jnp.clip(drawn, -reach, reach).astype(kind)


def setup_inputs(seed: int = 0) -> dict:
    seeds = jax.random.split(jax.random.key(seed), 10)
    return {
        "queries": draw_queries(jax.random.fold_in(seeds[9], 71), 0),
        "keys": draw_keys(jax.random.fold_in(seeds[9], 71), 0),
        "values": centred(seeds[2], (TOKENS, D), 1.0, 6.0, ((0, 8), (1, 4))),
        "residual": centred(seeds[3], (TOKENS, D), 0.5, 3.0, ((0, 8), (1, 4))),
        "reg_weight": centred(seeds[4], (D, TARGET_D), D ** -0.5, 0.1875, ((0, 4),)),
        "targets": centred(seeds[5], (TRACKS, POOL, TARGET_D), 0.5, 3.0, ((0, 8),)),
        "block_track": plant(skewed_ids(seeds[6], (BLOCKS,), TRACKS, 2), jax.random.fold_in(seeds[6], 3), 0, TRACKS - 1).astype(jnp.int32),
        "row_count": ragged_sizes(seeds[7], BLOCKS, 3 * BLK * BLOCKS // 4, BLK, 1).astype(jnp.int32),
        "pool_slot": plant(jax.random.randint(seeds[8], (BLOCKS, BLK), 0, POOL), jax.random.fold_in(seeds[8], 1), 0, POOL - 1).astype(jnp.int32),
    }


def attend(queries, keys, values):
    scale = HEAD_DIM ** -0.5
    block_size = min(512, TOKENS)
    query_heads = queries.reshape(TOKENS, HEADS, HEAD_DIM).transpose(1, 0, 2)
    key_heads = keys.reshape(TOKENS, HEADS, HEAD_DIM).transpose(1, 0, 2)
    value_heads = values.reshape(TOKENS, HEADS, HEAD_DIM).transpose(1, 0, 2)

    def per_head(operands):
        query_one, key_one, value_one = operands

        def per_block(query_block):
            scores = jnp.dot(query_block, key_one.T, preferred_element_type=jnp.float32) * scale
            largest = jnp.max(scores, axis=1, keepdims=True)
            exp_terms = jnp.exp(scores - largest)
            totals = jnp.sum(exp_terms, axis=1, keepdims=True)
            weighted = jnp.dot(exp_terms.astype(jnp.bfloat16), value_one, preferred_element_type=jnp.float32)
            return (weighted / totals).astype(jnp.bfloat16)

        blocks = query_one.reshape(TOKENS // block_size, block_size, HEAD_DIM)
        return lax.map(per_block, blocks).reshape(TOKENS, HEAD_DIM)

    context = lax.map(per_head, (query_heads, key_heads, value_heads))
    return context.transpose(1, 0, 2).reshape(TOKENS, D)


def reference(queries, keys, values, residual, reg_weight, targets, block_track, row_count, pool_slot):
    context = attend(queries, keys, values)
    stream = (residual.astype(jnp.float32) + context.astype(jnp.float32)).astype(jnp.bfloat16)
    stream_blocks = stream.reshape(BLOCKS, BLK, D).astype(jnp.float32)
    valid = jnp.arange(BLK, dtype=jnp.int32)[None, :] < row_count[:, None]
    match = pool_slot[:, None, :] == jnp.arange(POOL, dtype=jnp.int32)[None, :, None]
    selector = jnp.where(match & valid[:, None, :], 1.0, 0.0).astype(jnp.float32)
    pooled = jnp.einsum("bpr,brc->bpc", selector, stream_blocks, precision=lax.Precision.HIGHEST)
    slot_rows = jnp.sum(selector, axis=2)
    track_select = jnp.where(block_track[:, None] == jnp.arange(TRACKS, dtype=jnp.int32)[None, :], 1.0, 0.0).astype(jnp.float32)
    sums = jnp.einsum("bt,bpc->tpc", track_select, pooled, precision=lax.Precision.HIGHEST)
    counts = jnp.einsum("bt,bp->tp", track_select, slot_rows, precision=lax.Precision.HIGHEST)
    divisor = jnp.maximum(counts, 1.0)
    mean = (sums / divisor[:, :, None]).astype(jnp.bfloat16).reshape(TRACKS * POOL, D)
    prediction = jnp.dot(mean, reg_weight, preferred_element_type=jnp.float32)
    error = (prediction - targets.reshape(TRACKS * POOL, TARGET_D).astype(jnp.float32)).astype(jnp.bfloat16)
    grad_reg = jnp.dot(mean.T, error, preferred_element_type=jnp.float32).astype(jnp.bfloat16)
    mean_grad = jnp.dot(error, reg_weight.T, preferred_element_type=jnp.float32)
    track_grad = (mean_grad.reshape(TRACKS, POOL, D) / divisor[:, :, None]).astype(jnp.bfloat16)
    pooled_grad = jnp.einsum("bt,tpc->bpc", track_select, track_grad.astype(jnp.float32), precision=lax.Precision.HIGHEST)
    row_grad = jnp.einsum("bpr,bpc->brc", selector, pooled_grad, precision=lax.Precision.HIGHEST)
    context_grad = row_grad.reshape(TOKENS, D).astype(jnp.bfloat16)
    return grad_reg, context_grad
```

```python
import functools

import jax
import jax.numpy as jnp
from jax import lax
from jax.experimental import pallas as pl
from jax.experimental.pallas import tpu as pltpu
from jax.sharding import PartitionSpec as P

HEAD_DIM = 64
BLK = 128
POOL = 16
INFO = 16
BF = jnp.bfloat16
F32 = jnp.float32
MESH = pl.DeviceIdType.MESH
NT = (((1,), (1,)), ((), ()))
TN = (((0,), (0,)), ((), ()))


def drain(ref, sem):
    pltpu.make_async_copy(ref, ref, sem).wait()


def remote(src, dst, send, recv, seq, head):
    return pltpu.make_async_remote_copy(
        src_ref=src, dst_ref=dst, send_sem=send, recv_sem=recv,
        device_id={"seq": seq, "head": head}, device_id_type=MESH,
    )


def kernel(
    n, q_ref, k_ref, v_ref, r_ref, w_ref, tgt_ref, bt_ref, rc_ref, ps_ref,
    greg_ref, cgrad_ref,
    kvs, qrs, kvb, qrb, qx, vx, run_max, acc, wbuf, stream, sb, rb, ms, mb, es, eb, gacc,
    kv_send, kv_recv, qr_send, qr_recv, fw_send, w_send, w_recv,
    b_send, b_recv, m_send, m_recv, e_send, e_recv, ef_send, ef_recv,
):
    g = n // 8
    devices = 4 * n
    seq, head = lax.axis_index("seq"), lax.axis_index("head")
    core, yy = head % 2, head // 2
    partner, across = 2 * yy + 1 - core, (head + 2) % 4
    lin = seq * 4 + head
    tok = q_ref.shape[0]

    barrier = pltpu.get_barrier_semaphore()

    @pl.loop(1, devices)
    def _(i):
        other = (lin + i) % devices
        pl.semaphore_signal(
            barrier, inc=1, device_id={"seq": other // 4, "head": other % 4}, device_id_type=MESH
        )

    lane_row = lax.broadcasted_iota(jnp.int32, (1, BLK), 1)
    slots = [
        jnp.where(lane_row < rc_ref[b], ps_ref[b:b + 1, :], -1).astype(F32) for b in range(2)
    ]
    own_tracks = [bt_ref[2 * seq + b] for b in range(2)]
    row = lax.broadcasted_iota(jnp.int32, (INFO, BLK), 0)
    tracks = jnp.where(row == 2, own_tracks[0], own_tracks[1]).astype(F32)
    info = jnp.where(row == 0, slots[0], jnp.where(row == 1, slots[1], tracks)).astype(BF)
    for j in range(4):
        cols = slice(j * HEAD_DIM, (j + 1) * HEAD_DIM)
        qrs[j] = jnp.concatenate([q_ref[:, cols] * BF(HEAD_DIM ** -0.5), r_ref[:, cols]], axis=1)
        kvs[j, 0:tok, :] = jnp.concatenate([k_ref[:, cols], v_ref[:, cols]], axis=1)
        kvs[j, tok:tok + INFO, :] = info

    pl.semaphore_wait(barrier, devices - 1)

    half, chunk = (seq // 4) % 2, seq // 8
    to_head = 2 * yy + half

    def first_sends(act):
        for j in range(4):
            lead = (4 * core + j) * g
            here = jnp.logical_and(lead + chunk == seq, to_head == head)
            act(
                here,
                remote(qrs.at[j], qrb.at[seq % 4], qr_send.at[j], qr_recv, lead + chunk, to_head),
                pltpu.make_async_copy(qrs.at[j], qrb.at[seq % 4], qr_recv),
            )
            for c in range(g):
                here = jnp.logical_and(lead + c == seq, to_head == head)
                act(
                    here,
                    remote(kvs.at[j], kvb.at[seq], kv_send.at[j * g + c], kv_recv.at[seq],
                           lead + c, to_head),
                    pltpu.make_async_copy(kvs.at[j], kvb.at[seq], kv_recv.at[seq]),
                )

    def begin(here, far, near):
        @pl.when(here)
        def _():
            near.start()

        @pl.when(jnp.logical_not(here))
        def _():
            far.start()

    def finish(here, far, near):
        @pl.when(jnp.logical_not(here))
        def _():
            far.wait_send()

    first_sends(begin)
    w_across = remote(w_ref, wbuf.at[head], w_send.at[0], w_recv.at[head], seq, across)
    w_pair = remote(w_ref, wbuf.at[head], w_send.at[1], w_recv.at[head], seq, partner)
    w_own = pltpu.make_async_copy(w_ref, wbuf.at[head], w_recv.at[head])
    w_across.start()
    w_pair.start()
    w_own.start()

    run_max[...] = jnp.full_like(run_max, -1e30)
    acc[...] = jnp.zeros_like(acc)
    queries = qx.shape[0]
    low = lax.broadcasted_iota(jnp.int32, (1, 2 * HEAD_DIM), 1) < HEAD_DIM

    drain(qrb, qr_recv)
    flat = qrb[...].reshape(queries, 2 * HEAD_DIM)
    qx[...] = jnp.where(low, flat, jnp.zeros_like(flat))

    def attend(first):
        pair = kvb[pl.ds(first, 2), 0:tok, :].reshape(2 * tok, 2 * HEAD_DIM)
        vx[...] = jnp.where(low, jnp.ones_like(pair), pair)
        for t in range(queries // 256):
            rows = slice(t * 256, (t + 1) * 256)
            scores = lax.dot_general(qx[rows, :], pair, NT, preferred_element_type=F32)
            old = run_max[rows, :]
            new = jnp.maximum(old, jnp.max(scores, axis=1, keepdims=True))
            weights = jnp.exp(scores - new[:, 0:1]).astype(BF)
            acc[rows, :] = acc[rows, :] * jnp.exp(old - new) + jnp.dot(
                weights, vx[...], preferred_element_type=F32
            )
            run_max[rows, :] = new

    @pl.loop(0, n // 4)
    def _(i):
        first = (i // 2) * 8 + 4 * core + 2 * (i % 2)
        for one in range(2):
            s = first + one
            drain(kvb.at[s], kv_recv.at[s])
            remote(kvb.at[s], kvb.at[s], fw_send, kv_recv.at[s], seq, partner).start()
        attend(first)

    @pl.loop(0, n // 4)
    def _(i):
        first = (i // 2) * 8 + 4 * (1 - core) + 2 * (i % 2)
        for one in range(2):
            drain(kvb.at[first + one], kv_recv.at[first + one])
        attend(first)

    drain(wbuf.at[across], w_recv.at[across])
    w_on = remote(wbuf.at[across], wbuf.at[across], w_send.at[2], w_recv.at[across], seq, partner)
    w_on.start()

    def codes_of(s):
        lines = kvb[s, tok:tok + INFO, :].astype(F32)
        return [
            jnp.where(lines[b:b + 1] < 0, -1.0, POOL * lines[2 + b:3 + b] + lines[b:b + 1])
            for b in range(2)
        ]

    total = acc[...]
    context = (total / pltpu.roll(total, HEAD_DIM, 1)).astype(BF).astype(F32)
    summed = (qrb[...].reshape(queries, 2 * HEAD_DIM).astype(F32) + context).astype(BF)
    stream[...] = jnp.where(low, jnp.zeros_like(summed), summed)

    here_first = (seq % g) * 8 + 4 * core
    here_codes = [code for i in range(4) for code in codes_of(here_first + i)]
    big_rows = lax.broadcasted_iota(jnp.int32, (512, BLK), 0).astype(F32)

    @pl.loop(0, devices // 32)
    def _(i):
        base = (i * 512).astype(F32)
        pick = jnp.concatenate(
            [jnp.where(big_rows == code - base, 1.0, 0.0).astype(BF) for code in here_codes],
            axis=1,
        )
        part = jnp.dot(pick, stream[...], preferred_element_type=F32)
        part = part.reshape(32, POOL, 2 * HEAD_DIM)
        upper, lower = part[:, 0:8, :], part[:, 8:16, :]
        turned = pltpu.roll(lower.reshape(256, 2 * HEAD_DIM), HEAD_DIM, 1)
        sb[pl.ds(i * 32, 32)] = jnp.where(low, turned, upper.reshape(256, 2 * HEAD_DIM)).reshape(
            32, 8, 2 * HEAD_DIM
        )

    @pl.loop(1, devices)
    def _(i):
        t = (lin + i) % devices
        remote(sb.at[t], rb.at[lin], b_send, b_recv, t // 4, t % 4).start()

    pltpu.make_async_copy(sb.at[lin], rb.at[lin], b_recv).start()

    slot_row = lax.broadcasted_iota(jnp.int32, (POOL, BLK), 0)
    wanted = [(t * POOL + slot_row).astype(F32) for t in (lin, own_tracks[0], own_tracks[1])]

    def add_counts(s, sums):
        codes = codes_of(s)
        return tuple(
            total + jnp.where(want == codes[0], 1.0, 0.0) + jnp.where(want == codes[1], 1.0, 0.0)
            for total, want in zip(sums, wanted)
        )

    zero = jnp.zeros((POOL, BLK), F32)
    counts = lax.fori_loop(0, n, add_counts, (zero, zero, zero))
    divisors = [jnp.maximum(jnp.sum(c, axis=1, keepdims=True), 1.0) for c in counts]

    drain(rb, b_recv)
    tiles = []
    for pair in range(8):
        sides = []
        for hd in (2 * pair, 2 * pair + 1):
            y, h = hd // 8, hd % 8
            side = None
            for c in range(2):
                for part in range(g):
                    piece = rb[(h * g + part) * 4 + 2 * y + c]
                    side = piece if side is None else side + piece
            sides.append(side)
        a, b = sides
        upper = jnp.where(low, pltpu.roll(a, HEAD_DIM, 1), b)
        lower = jnp.where(low, a, pltpu.roll(b, HEAD_DIM, 1))
        tiles.append((jnp.concatenate([upper, lower], axis=0) / divisors[0]).astype(BF))
    for k in range(4):
        ms[k] = jnp.concatenate(tiles[2 * k:2 * k + 2], axis=1)

    place = core * 2 * n + seq * 2 + yy

    @pl.loop(1, devices)
    def _(i):
        t = (lin + i) % devices
        remote(ms.at[t % 4], mb.at[place], m_send, m_recv, t // 4, t % 4).start()

    pltpu.make_async_copy(ms.at[head], mb.at[place], m_recv).start()

    for k in range(2):
        drain(wbuf.at[2 * yy + k], w_recv.at[2 * yy + k])
    drain(wbuf.at[2 * (1 - yy) + 1 - core], w_recv.at[2 * (1 - yy) + 1 - core])
    prediction = jnp.dot(ms[0], wbuf[0], preferred_element_type=F32)
    for k in range(1, 4):
        prediction += jnp.dot(ms[k], wbuf[k], preferred_element_type=F32)
    es[...] = (prediction - tgt_ref[head].astype(F32)).astype(BF)

    @pl.loop(1, 2 * n)
    def _(i):
        spot = (seq * 2 + yy + i) % (2 * n)
        remote(es, eb.at[place], e_send, e_recv, spot // 2, 2 * (spot % 2) + core).start()

    pltpu.make_async_copy(es, eb.at[place], e_recv).start()

    drain(mb, m_recv)
    mine, theirs = pl.ds(core * 2 * n, 2 * n), pl.ds((1 - core) * 2 * n, 2 * n)
    drain(eb.at[mine], e_recv)
    e_on = remote(eb.at[mine], eb.at[mine], ef_send, ef_recv, seq, partner)
    e_on.start()

    own_code = jnp.concatenate(
        [(t * POOL + lax.broadcasted_iota(jnp.int32, (POOL, 1), 0)) for t in own_tracks], axis=0
    )
    picked = jnp.zeros((2 * POOL, es.shape[1]), F32)
    for turn in range(2):
        side = core if turn == 0 else 1 - core
        if turn == 1:
            drain(eb.at[theirs], ef_recv)

        def gather(i, picked, side=side, fresh=turn == 0):
            begin_at = side * 2 * n + i * 16
            means = mb[pl.ds(begin_at, 16)].reshape(256, -1)
            errors = eb[pl.ds(begin_at, 16)].reshape(256, -1)
            term = lax.dot_general(means, errors, TN, preferred_element_type=F32)
            if fresh:
                gacc[...] = term + jnp.where(i > 0, gacc[...], 0.0)
            else:
                gacc[...] += term
            spot = lax.broadcasted_iota(jnp.int32, (2 * POOL, 256), 1)
            where = i * 16 + spot // POOL
            code = (2 * where + side) * POOL + spot % POOL
            pick = jnp.where(code == own_code, 1.0, 0.0).astype(BF)
            return picked + jnp.dot(pick, errors, preferred_element_type=F32)

        picked = lax.fori_loop(0, n // 8, gather, picked)

    greg_ref[...] = gacc[...].astype(BF)
    mean_grad = lax.dot_general(picked.astype(BF), w_ref[...], NT, preferred_element_type=F32)
    track_grad = (mean_grad / jnp.concatenate(divisors[1:], axis=0)).astype(BF)
    for b in range(2):
        select = jnp.where(slot_row.astype(F32) == slots[b], 1.0, 0.0).astype(BF)
        cgrad_ref[b * BLK:(b + 1) * BLK, :] = lax.dot_general(
            select, track_grad[b * POOL:(b + 1) * POOL], TN, preferred_element_type=F32
        ).astype(BF)

    first_sends(finish)
    drain(kvb.at[pl.ds(0, n // 2)], fw_send)
    w_across.wait_send()
    w_pair.wait_send()
    w_on.wait_send()
    drain(sb.at[pl.ds(0, devices - 1)], b_send)
    drain(mb.at[pl.ds(0, devices - 1)], m_send)
    drain(eb.at[pl.ds(0, 2 * n - 1)], e_send)
    e_on.wait_send()


def solution(mesh):
    n = mesh.shape["seq"]
    devices = 4 * n

    def local(queries, keys, values, residual, weight, targets, block_track, row_count, slot):
        tok, width = queries.shape
        target_width = weight.shape[1]
        dma = pltpu.SemaphoreType.DMA
        vmem, smem = pl.BlockSpec(memory_space=pltpu.VMEM), pl.BlockSpec(memory_space=pltpu.SMEM)
        two = 2 * HEAD_DIM
        return pl.pallas_call(
            functools.partial(kernel, n),
            out_shape=(
                jax.ShapeDtypeStruct((width, target_width), BF),
                jax.ShapeDtypeStruct((tok, width), BF),
            ),
            in_specs=[vmem] * 6 + [smem, smem, vmem],
            out_specs=(vmem, vmem),
            scratch_shapes=[
                pltpu.VMEM((4, tok + INFO, two), BF),
                pltpu.VMEM((4, tok, two), BF),
                pltpu.VMEM((n, tok + INFO, two), BF),
                pltpu.VMEM((4, tok, two), BF),
                pltpu.VMEM((4 * tok, two), BF),
                pltpu.VMEM((2 * tok, two), BF),
                pltpu.VMEM((4 * tok, two), F32),
                pltpu.VMEM((4 * tok, two), F32),
                pltpu.VMEM((4, width, target_width), BF),
                pltpu.VMEM((4 * tok, two), BF),
                pltpu.VMEM((devices, 8, two), F32),
                pltpu.VMEM((devices, 8, two), F32),
                pltpu.VMEM((4, POOL, width), BF),
                pltpu.VMEM((devices, POOL, width), BF),
                pltpu.VMEM((POOL, target_width), BF),
                pltpu.VMEM((devices, POOL, target_width), BF),
                pltpu.VMEM((width, target_width), F32),
                dma((4 * (n // 8),)),
                dma((n,)),
                dma((4,)),
                dma,
                dma,
                dma((3,)),
                dma((4,)),
                dma, dma, dma, dma, dma, dma, dma, dma,
            ],
            compiler_params=pltpu.CompilerParams(
                collective_id=0, has_side_effects=True, vmem_limit_bytes=56 * 1024 * 1024
            ),
            cost_estimate=pl.CostEstimate(
                flops=4 * 4 * tok * n * tok * HEAD_DIM, bytes_accessed=8 * 1024 * 1024,
                transcendentals=4 * tok * n * tok,
            ),
        )(queries, keys, values, residual, weight, targets, block_track, row_count, slot)

    return jax.shard_map(
        local,
        mesh=mesh,
        in_specs=(
            P("seq", "head"),
            P("seq", "head"),
            P("seq", "head"),
            P("seq", "head"),
            P("head", None),
            P("seq", None, None),
            P(),
            P("seq"),
            P("seq", None),
        ),
        out_specs=(P("head", None), P("seq", "head")),
        check_vma=False,
    )
```

```python
import functools

import jax
import jax.numpy as jnp
from jax import lax
from jax.experimental import pallas as pl
from jax.experimental.pallas import tpu as pltpu
from jax.sharding import PartitionSpec as P

HEAD_DIM = 64
BLK = 128
POOL = 16
INFO = 16
BF = jnp.bfloat16
F32 = jnp.float32
MESH = pl.DeviceIdType.MESH
NT = (((1,), (1,)), ((), ()))
TN = (((0,), (0,)), ((), ()))


def drain(ref, sem):
    pltpu.make_async_copy(ref, ref, sem).wait()


def remote(src, dst, send, recv, seq, head):
    return pltpu.make_async_remote_copy(
        src_ref=src, dst_ref=dst, send_sem=send, recv_sem=recv,
        device_id={"seq": seq, "head": head}, device_id_type=MESH,
    )


def kernel(
    n, q_ref, k_ref, v_ref, r_ref, w_ref, tgt_ref, bt_ref, rc_ref, ps_ref,
    greg_ref, cgrad_ref,
    kvs, qrs, kvb, qrb, qx, vx, run_max, acc, wbuf, stream, sb, rb, m1, mb, eb, gacc,
    kv_send, kv_recv, qr_send, qr_recv, fw_send, w_send, w_recv,
    b_send, b_recv, m_send, m_recv, m2_send, m2_recv, e_send, e_recv, e2_send, e2_recv,
    ef_send, ef_recv,
):
    g = n // 8
    devices = 4 * n
    seq, head = lax.axis_index("seq"), lax.axis_index("head")
    core, yy = head % 2, head // 2
    partner, across = 2 * yy + 1 - core, (head + 2) % 4
    lin = seq * 4 + head
    tok = q_ref.shape[0]

    barrier = pltpu.get_barrier_semaphore()

    @pl.loop(1, devices)
    def _(i):
        other = (lin + i) % devices
        pl.semaphore_signal(
            barrier, inc=1, device_id={"seq": other // 4, "head": other % 4}, device_id_type=MESH
        )

    lane_row = lax.broadcasted_iota(jnp.int32, (1, BLK), 1)
    slots = [
        jnp.where(lane_row < rc_ref[b], ps_ref[b:b + 1, :], -1).astype(F32) for b in range(2)
    ]
    own_tracks = [bt_ref[2 * seq + b] for b in range(2)]
    row = lax.broadcasted_iota(jnp.int32, (INFO, BLK), 0)
    tracks = jnp.where(row == 2, own_tracks[0], own_tracks[1]).astype(F32)
    info = jnp.where(row == 0, slots[0], jnp.where(row == 1, slots[1], tracks)).astype(BF)
    for j in range(4):
        cols = slice(j * HEAD_DIM, (j + 1) * HEAD_DIM)
        qrs[j] = jnp.concatenate([q_ref[:, cols] * BF(HEAD_DIM ** -0.5), r_ref[:, cols]], axis=1)
        kvs[j, 0:tok, :] = jnp.concatenate([k_ref[:, cols], v_ref[:, cols]], axis=1)
        kvs[j, tok:tok + INFO, :] = info

    pl.semaphore_wait(barrier, devices - 1)

    half, chunk = (seq // 4) % 2, seq // 8
    to_head = 2 * yy + half

    def first_sends(act):
        for j in range(4):
            lead = (4 * core + j) * g
            act(
                jnp.logical_and(lead + chunk == seq, to_head == head),
                remote(qrs.at[j], qrb.at[seq % 4], qr_send.at[j], qr_recv, lead + chunk, to_head),
                pltpu.make_async_copy(qrs.at[j], qrb.at[seq % 4], qr_recv),
            )
        for j in range(4):
            lead = (4 * core + j) * g
            for c in range(g):
                act(
                    jnp.logical_and(lead + c == seq, to_head == head),
                    remote(kvs.at[j], kvb.at[seq], kv_send.at[j * g + c], kv_recv.at[seq],
                           lead + c, to_head),
                    pltpu.make_async_copy(kvs.at[j], kvb.at[seq], kv_recv.at[seq]),
                )

    def begin(here, far, near):
        @pl.when(here)
        def _():
            near.start()

        @pl.when(jnp.logical_not(here))
        def _():
            far.start()

    def finish(here, far, near):
        @pl.when(jnp.logical_not(here))
        def _():
            far.wait_send()

    first_sends(begin)
    w_across = remote(w_ref, wbuf.at[head], w_send.at[0], w_recv.at[head], seq, across)
    w_pair = remote(w_ref, wbuf.at[head], w_send.at[1], w_recv.at[head], seq, partner)
    w_own = pltpu.make_async_copy(w_ref, wbuf.at[head], w_recv.at[head])
    w_across.start()
    w_pair.start()
    w_own.start()

    run_max[...] = jnp.full_like(run_max, -1e30)
    acc[...] = jnp.zeros_like(acc)
    queries = qx.shape[0]
    low = lax.broadcasted_iota(jnp.int32, (1, 2 * HEAD_DIM), 1) < HEAD_DIM

    drain(qrb, qr_recv)
    flat = qrb[...].reshape(queries, 2 * HEAD_DIM)
    qx[...] = jnp.where(low, flat, jnp.zeros_like(flat))

    def attend(first):
        pair = kvb[pl.ds(first, 2), 0:tok, :].reshape(2 * tok, 2 * HEAD_DIM)
        vx[...] = jnp.where(low, jnp.ones_like(pair), pair)
        for t in range(queries // 256):
            rows = slice(t * 256, (t + 1) * 256)
            scores = lax.dot_general(qx[rows, :], pair, NT, preferred_element_type=F32)
            old = run_max[rows, :]
            new = jnp.maximum(old, jnp.max(scores, axis=1, keepdims=True))
            weights = jnp.exp(scores - new[:, 0:1]).astype(BF)
            acc[rows, :] = acc[rows, :] * jnp.exp(old - new) + jnp.dot(
                weights, vx[...], preferred_element_type=F32
            )
            run_max[rows, :] = new

    @pl.loop(0, n // 4)
    def _(i):
        first = (i // 2) * 8 + 4 * core + 2 * (i % 2)
        for one in range(2):
            s = first + one
            drain(kvb.at[s], kv_recv.at[s])
            remote(kvb.at[s], kvb.at[s], fw_send, kv_recv.at[s], seq, partner).start()
        attend(first)

    @pl.loop(0, n // 4)
    def _(i):
        first = (i // 2) * 8 + 4 * (1 - core) + 2 * (i % 2)
        for one in range(2):
            drain(kvb.at[first + one], kv_recv.at[first + one])
        attend(first)

    drain(wbuf.at[across], w_recv.at[across])
    w_on = remote(wbuf.at[across], wbuf.at[across], w_send.at[2], w_recv.at[across], seq, partner)
    w_on.start()

    def codes_of(s):
        lines = kvb[s, tok:tok + INFO, :].astype(F32)
        return [
            jnp.where(lines[b:b + 1] < 0, -1.0, POOL * lines[2 + b:3 + b] + lines[b:b + 1])
            for b in range(2)
        ]

    total = acc[...]
    context = (total / pltpu.roll(total, HEAD_DIM, 1)).astype(BF).astype(F32)
    summed = (qrb[...].reshape(queries, 2 * HEAD_DIM).astype(F32) + context).astype(BF)
    stream[...] = jnp.where(low, jnp.zeros_like(summed), summed)

    here_first = (seq % g) * 8 + 4 * core
    here_codes = [code for i in range(4) for code in codes_of(here_first + i)]
    big_rows = lax.broadcasted_iota(jnp.int32, (512, BLK), 0).astype(F32)

    @pl.loop(0, devices // 32)
    def _(i):
        base = (i * 512).astype(F32)
        pick = jnp.concatenate(
            [jnp.where(big_rows == code - base, 1.0, 0.0).astype(BF) for code in here_codes],
            axis=1,
        )
        part = jnp.dot(pick, stream[...], preferred_element_type=F32)
        part = part.reshape(32, POOL, 2 * HEAD_DIM)
        upper, lower = part[:, 0:8, :], part[:, 8:16, :]
        turned = pltpu.roll(lower.reshape(256, 2 * HEAD_DIM), HEAD_DIM, 1)
        sb[pl.ds(i * 32, 32)] = jnp.where(low, turned, upper.reshape(256, 2 * HEAD_DIM)).reshape(
            32, 8, 2 * HEAD_DIM
        )

    @pl.loop(1, devices)
    def _(i):
        t = (lin + i) % devices
        remote(sb.at[t], rb.at[lin], b_send, b_recv, t // 4, t % 4).start()

    pltpu.make_async_copy(sb.at[lin], rb.at[lin], b_recv).start()

    slot_row = lax.broadcasted_iota(jnp.int32, (POOL, BLK), 0)
    wanted = [(t * POOL + slot_row).astype(F32) for t in (lin, own_tracks[0], own_tracks[1])]

    def add_counts(s, sums):
        codes = codes_of(s)
        return tuple(
            total + jnp.where(want == codes[0], 1.0, 0.0) + jnp.where(want == codes[1], 1.0, 0.0)
            for total, want in zip(sums, wanted)
        )

    zero = jnp.zeros((POOL, BLK), F32)
    counts = lax.fori_loop(0, n, add_counts, (zero, zero, zero))
    divisors = [jnp.maximum(jnp.sum(c, axis=1, keepdims=True), 1.0) for c in counts]

    drain(rb, b_recv)
    tiles = []
    for pair in range(8):
        sides = []
        for hd in (2 * pair, 2 * pair + 1):
            y, h = hd // 8, hd % 8
            side = None
            for c in range(2):
                for part in range(g):
                    piece = rb[(h * g + part) * 4 + 2 * y + c]
                    side = piece if side is None else side + piece
            sides.append(side)
        a, b = sides
        upper = jnp.where(low, pltpu.roll(a, HEAD_DIM, 1), b)
        lower = jnp.where(low, a, pltpu.roll(b, HEAD_DIM, 1))
        tiles.append((jnp.concatenate([upper, lower], axis=0) / divisors[0]).astype(BF))
    line = n // 2
    outer, inner = seq // 2, seq % 2
    sign = 1 - 2 * (outer // (line // 2))
    block = inner * 2 + yy
    mean = [jnp.concatenate(tiles[2 * k:2 * k + 2], axis=1) for k in range(4)]
    for k in range(4):
        m1[k, outer] = mean[k]

    def along(i):
        return (outer + sign * i + line) % line

    def plane(d):
        return (inner + d % 2) % 2, (yy + d // 2) % 2

    @pl.loop(1, line)
    def _(i):
        spot = m1.at[:, outer]
        remote(spot, spot, m_send, m_recv, along(i) * 2 + inner, head).start()

    for k in range(2):
        drain(wbuf.at[2 * yy + k], w_recv.at[2 * yy + k])
    drain(wbuf.at[2 * (1 - yy) + 1 - core], w_recv.at[2 * (1 - yy) + 1 - core])
    prediction = jnp.dot(mean[0], wbuf[0], preferred_element_type=F32)
    for k in range(1, 4):
        prediction += jnp.dot(mean[k], wbuf[k], preferred_element_type=F32)
    error_at = eb.at[core, block * line + outer]
    error_at[...] = (prediction - tgt_ref[head].astype(F32)).astype(BF)

    @pl.loop(1, line)
    def _(i):
        remote(
            error_at, error_at, e_send, e_recv.at[outer], along(i) * 2 + inner, head
        ).start()

    drain(m1.at[:, 0:line - 1], m_recv)
    mean_to = mb.at[core, pl.ds(block * line, line)]
    for d in range(4):
        to_inner, to_yy = plane(d)
        for c in range(2):
            to = 2 * to_yy + (core if c == 0 else 1 - core)
            if d == 0 and c == 0:
                pltpu.make_async_copy(m1.at[to], mean_to, m2_recv).start()
            else:
                remote(m1.at[to], mean_to, m2_send, m2_recv, outer * 2 + to_inner, to).start()

    @pl.loop(0, line)
    def _(i):
        spot = block * line + along(i)

        @pl.when(i > 0)
        def _():
            drain(eb.at[core, spot], e_recv.at[along(i)])

        for d in range(1, 4):
            to_inner, to_yy = plane(d)
            remote(
                eb.at[core, spot], eb.at[core, spot], e2_send, e2_recv.at[block],
                outer * 2 + to_inner, 2 * to_yy + core,
            ).start()

    for d in range(4):
        from_inner, from_yy = plane(d)
        other = from_inner * 2 + from_yy
        part = eb.at[core, pl.ds(other * line, line)]
        if d > 0:
            drain(part, e2_recv.at[other])
        remote(part, part, ef_send, ef_recv.at[other], seq, partner).start()

    drain(mb, m2_recv)

    own_code = jnp.concatenate(
        [(t * POOL + lax.broadcasted_iota(jnp.int32, (POOL, 1), 0)) for t in own_tracks], axis=0
    )
    picked = jnp.zeros((2 * POOL, w_ref.shape[1]), F32)
    for turn in range(2):
        side = core if turn == 0 else 1 - core
        if turn == 1:
            for o in range(4):
                drain(eb.at[side, pl.ds(o * line, line)], ef_recv.at[o])

        def gather(i, picked, side=side, fresh=turn == 0):
            means = mb[side, pl.ds(i * 16, 16)].reshape(256, -1)
            errors = eb[side, pl.ds(i * 16, 16)].reshape(256, -1)
            term = lax.dot_general(means, errors, TN, preferred_element_type=F32)
            if fresh:
                gacc[...] = term + jnp.where(i > 0, gacc[...], 0.0)
            else:
                gacc[...] += term
            spot = lax.broadcasted_iota(jnp.int32, (2 * POOL, 256), 1)
            where = i * 16 + spot // POOL
            track = 4 * (2 * (where % line) + where // (2 * line)) + 2 * (where // line % 2) + side
            code = track * POOL + spot % POOL
            pick = jnp.where(code == own_code, 1.0, 0.0).astype(BF)
            return picked + jnp.dot(pick, errors, preferred_element_type=F32)

        picked = lax.fori_loop(0, n // 8, gather, picked)

    greg_ref[...] = gacc[...].astype(BF)
    mean_grad = lax.dot_general(picked.astype(BF), w_ref[...], NT, preferred_element_type=F32)
    track_grad = (mean_grad / jnp.concatenate(divisors[1:], axis=0)).astype(BF)
    for b in range(2):
        select = jnp.where(slot_row.astype(F32) == slots[b], 1.0, 0.0).astype(BF)
        cgrad_ref[b * BLK:(b + 1) * BLK, :] = lax.dot_general(
            select, track_grad[b * POOL:(b + 1) * POOL], TN, preferred_element_type=F32
        ).astype(BF)

    first_sends(finish)
    drain(kvb.at[pl.ds(0, n // 2)], fw_send)
    w_across.wait_send()
    w_pair.wait_send()
    w_on.wait_send()
    drain(sb.at[pl.ds(0, devices - 1)], b_send)
    drain(m1.at[:, 0:line - 1], m_send)
    drain(eb.at[0, 0:7 * line // 4], m2_send)
    drain(eb.at[0, 0:line - 1], e_send)
    drain(eb.at[0, 0:3 * line], e2_send)
    drain(eb.at[0], ef_send)


def solution(mesh):
    n = mesh.shape["seq"]
    devices = 4 * n

    def local(queries, keys, values, residual, weight, targets, block_track, row_count, slot):
        tok, width = queries.shape
        target_width = weight.shape[1]
        dma = pltpu.SemaphoreType.DMA
        vmem, smem = pl.BlockSpec(memory_space=pltpu.VMEM), pl.BlockSpec(memory_space=pltpu.SMEM)
        two = 2 * HEAD_DIM
        return pl.pallas_call(
            functools.partial(kernel, n),
            out_shape=(
                jax.ShapeDtypeStruct((width, target_width), BF),
                jax.ShapeDtypeStruct((tok, width), BF),
            ),
            in_specs=[vmem] * 6 + [smem, smem, vmem],
            out_specs=(vmem, vmem),
            scratch_shapes=[
                pltpu.VMEM((4, tok + INFO, two), BF),
                pltpu.VMEM((4, tok, two), BF),
                pltpu.VMEM((n, tok + INFO, two), BF),
                pltpu.VMEM((4, tok, two), BF),
                pltpu.VMEM((4 * tok, two), BF),
                pltpu.VMEM((2 * tok, two), BF),
                pltpu.VMEM((4 * tok, two), F32),
                pltpu.VMEM((4 * tok, two), F32),
                pltpu.VMEM((4, width, target_width), BF),
                pltpu.VMEM((4 * tok, two), BF),
                pltpu.VMEM((devices, 8, two), F32),
                pltpu.VMEM((devices, 8, two), F32),
                pltpu.VMEM((4, n // 2, POOL, width), BF),
                pltpu.VMEM((2, 2 * n, POOL, width), BF),
                pltpu.VMEM((2, 2 * n, POOL, target_width), BF),
                pltpu.VMEM((width, target_width), F32),
                dma((4 * (n // 8),)),
                dma((n,)),
                dma((4,)),
                dma,
                dma,
                dma((3,)),
                dma((4,)),
                dma, dma, dma, dma, dma, dma,
                dma, dma((n // 2,)), dma, dma((4,)), dma, dma((4,)),
            ],
            compiler_params=pltpu.CompilerParams(
                collective_id=0, has_side_effects=True, vmem_limit_bytes=56 * 1024 * 1024
            ),
            cost_estimate=pl.CostEstimate(
                flops=4 * 4 * tok * n * tok * HEAD_DIM, bytes_accessed=8 * 1024 * 1024,
                transcendentals=4 * tok * n * tok,
            ),
        )(queries, keys, values, residual, weight, targets, block_track, row_count, slot)

    return jax.shard_map(
        local,
        mesh=mesh,
        in_specs=(
            P("seq", "head"),
            P("seq", "head"),
            P("seq", "head"),
            P("seq", "head"),
            P("head", None),
            P("seq", None, None),
            P(),
            P("seq"),
            P("seq", None),
        ),
        out_specs=(P("head", None), P("seq", "head")),
        check_vma=False,
    )
```

```python
import functools

import jax
import jax.numpy as jnp
from jax import lax
from jax.experimental import pallas as pl
from jax.experimental.pallas import tpu as pltpu
from jax.sharding import PartitionSpec as P

HEAD_DIM = 64
BLK = 128
POOL = 16
INFO = 16
BF = jnp.bfloat16
F32 = jnp.float32
MESH = pl.DeviceIdType.MESH
NT = (((1,), (1,)), ((), ()))
TN = (((0,), (0,)), ((), ()))


def drain(ref, sem):
    pltpu.make_async_copy(ref, ref, sem).wait()


def remote(src, dst, send, recv, seq, head):
    return pltpu.make_async_remote_copy(
        src_ref=src, dst_ref=dst, send_sem=send, recv_sem=recv,
        device_id={"seq": seq, "head": head}, device_id_type=MESH,
    )


def kernel(
    n, q_ref, k_ref, v_ref, r_ref, w_ref, tgt_ref, bt_ref, rc_ref, ps_ref,
    greg_ref, tgrad_ref,
    kvs, qs, rs, kvb, qb, rb_in, qx, rx, vxt, run_max, acc, wbuf, sb, rb, m1, mb, eb, gacc,
    kv_send, kv_recv, q_send, q_recv, r_send, r_recv, fw_send, w_send, w_recv,
    b_send, b_recv, m_send, m_recv, m2_send, m2_recv, e_send, e_recv, e2_send, e2_recv,
    ef_send, ef_recv,
):
    g = n // 8
    devices = 4 * n
    seq, head = lax.axis_index("seq"), lax.axis_index("head")
    core, yy = head % 2, head // 2
    partner, across = 2 * yy + 1 - core, (head + 2) % 4
    lin = seq * 4 + head
    tok = q_ref.shape[0]

    barrier = pltpu.get_barrier_semaphore()

    @pl.loop(1, devices)
    def _(i):
        other = (lin + i) % devices
        pl.semaphore_signal(
            barrier, inc=1, device_id={"seq": other // 4, "head": other % 4}, device_id_type=MESH
        )

    lane_row = lax.broadcasted_iota(jnp.int32, (1, BLK), 1)
    slots = [
        jnp.where(lane_row < rc_ref[b], ps_ref[b:b + 1, :], -1).astype(F32) for b in range(2)
    ]
    own_tracks = [bt_ref[2 * seq + b] for b in range(2)]
    row = lax.broadcasted_iota(jnp.int32, (INFO, BLK), 0)
    tracks = jnp.where(row == 2, own_tracks[0], own_tracks[1]).astype(F32)
    info = jnp.where(row == 0, slots[0], jnp.where(row == 1, slots[1], tracks)).astype(BF)
    for j in range(4):
        cols = slice(j * HEAD_DIM, (j + 1) * HEAD_DIM)
        qs[j] = jnp.concatenate([q_ref[0:BLK, cols], q_ref[BLK:, cols]], axis=1) * BF(HEAD_DIM ** -0.5)
        rs[j] = jnp.concatenate([r_ref[0:BLK, cols], r_ref[BLK:, cols]], axis=1)
        kvs[j, 0:tok, :] = jnp.concatenate([k_ref[:, cols], v_ref[:, cols]], axis=1)
        kvs[j, tok:tok + INFO, :] = info

    pl.semaphore_wait(barrier, devices - 1)

    half, chunk = (seq // 4) % 2, seq // 8
    to_head = 2 * yy + half

    def first_sends(act):
        def whole(src, dst, send, recv):
            for j in range(4):
                lead = (4 * core + j) * g + chunk
                act(
                    jnp.logical_and(lead == seq, to_head == head),
                    remote(src.at[j], dst.at[seq % 4], send.at[j], recv, lead, to_head),
                    pltpu.make_async_copy(src.at[j], dst.at[seq % 4], recv),
                )

        whole(qs, qb, q_send, q_recv)
        for j in range(4):
            lead = (4 * core + j) * g
            for c in range(g):
                act(
                    jnp.logical_and(lead + c == seq, to_head == head),
                    remote(kvs.at[j], kvb.at[seq], kv_send.at[j * g + c], kv_recv.at[seq],
                           lead + c, to_head),
                    pltpu.make_async_copy(kvs.at[j], kvb.at[seq], kv_recv.at[seq]),
                )
        whole(rs, rb_in, r_send, r_recv)

    def begin(here, far, near):
        @pl.when(here)
        def _():
            near.start()

        @pl.when(jnp.logical_not(here))
        def _():
            far.start()

    def finish(here, far, near):
        @pl.when(jnp.logical_not(here))
        def _():
            far.wait_send()

    first_sends(begin)
    w_across = remote(w_ref, wbuf.at[head], w_send.at[0], w_recv.at[head], seq, across)
    w_pair = remote(w_ref, wbuf.at[head], w_send.at[1], w_recv.at[head], seq, partner)
    w_own = pltpu.make_async_copy(w_ref, wbuf.at[head], w_recv.at[head])
    w_across.start()
    w_pair.start()
    w_own.start()

    run_max[...] = jnp.full_like(run_max, -1e30)
    acc[...] = jnp.zeros_like(acc)
    queries = qx.shape[0]
    low = lax.broadcasted_iota(jnp.int32, (1, 2 * HEAD_DIM), 1) < HEAD_DIM

    def unpack(src, dst, keep):
        for i in range(4):
            both = src[i].astype(F32)
            turned = pltpu.roll(both, HEAD_DIM, 1)
            first, second = (both, turned) if keep else (turned, both)
            mask = low if keep else jnp.logical_not(low)
            dst[2 * i * BLK:(2 * i + 1) * BLK, :] = jnp.where(mask, first, 0.0).astype(BF)
            dst[(2 * i + 1) * BLK:(2 * i + 2) * BLK, :] = jnp.where(mask, second, 0.0).astype(BF)

    drain(qb, q_recv)
    unpack(qb, qx, True)

    def attend(first):
        pair = kvb[pl.ds(first, 2), 0:tok, :].reshape(2 * tok, 2 * HEAD_DIM)
        vxt[...] = jnp.where(low, jnp.ones_like(pair), pair).T
        for t in range(queries // 256):
            cols = slice(t * 256, (t + 1) * 256)
            scores = lax.dot_general(pair, qx[cols, :], NT, preferred_element_type=F32)
            old = run_max[:, cols]
            new = jnp.maximum(old, jnp.max(scores, axis=0, keepdims=True))
            weights = jnp.exp(scores - new).astype(BF)
            acc[:, cols] = acc[:, cols] * jnp.exp(old - new) + jnp.dot(
                vxt[...], weights, preferred_element_type=F32
            )
            run_max[:, cols] = new

    @pl.loop(0, n // 4)
    def _(i):
        first = (i // 2) * 8 + 4 * core + 2 * (i % 2)
        for one in range(2):
            s = first + one
            drain(kvb.at[s], kv_recv.at[s])
            remote(kvb.at[s], kvb.at[s], fw_send, kv_recv.at[s], seq, partner).start()
        attend(first)

    @pl.loop(0, n // 4)
    def _(i):
        first = (i // 2) * 8 + 4 * (1 - core) + 2 * (i % 2)
        for one in range(2):
            drain(kvb.at[first + one], kv_recv.at[first + one])
        attend(first)

    drain(wbuf.at[across], w_recv.at[across])
    w_on = remote(wbuf.at[across], wbuf.at[across], w_send.at[2], w_recv.at[across], seq, partner)
    w_on.start()

    def codes_of(s):
        lines = kvb[s, tok:tok + INFO, :].astype(F32)
        return [
            jnp.where(lines[b:b + 1] < 0, -1.0, POOL * lines[2 + b:3 + b] + lines[b:b + 1])
            for b in range(2)
        ]

    context = (acc[HEAD_DIM:, :] / acc[0:HEAD_DIM, :]).astype(BF)
    context = jnp.concatenate([jnp.zeros_like(context), context], axis=0)
    drain(rb_in, r_recv)
    unpack(rb_in, rx, False)

    here_first = (seq % g) * 8 + 4 * core
    here_codes = [code for i in range(4) for code in codes_of(here_first + i)]
    big_rows = lax.broadcasted_iota(jnp.int32, (512, BLK), 0).astype(F32)

    @pl.loop(0, devices // 32)
    def _(i):
        base = (i * 512).astype(F32)
        pick = jnp.concatenate(
            [jnp.where(big_rows == code - base, 1.0, 0.0).astype(BF) for code in here_codes],
            axis=1,
        )
        part = jnp.dot(pick, rx[...], preferred_element_type=F32) + lax.dot_general(
            pick, context, NT, preferred_element_type=F32
        )
        part = part.reshape(32, POOL, 2 * HEAD_DIM)
        upper, lower = part[:, 0:8, :], part[:, 8:16, :]
        turned = pltpu.roll(lower.reshape(256, 2 * HEAD_DIM), HEAD_DIM, 1)
        sb[pl.ds(i * 32, 32)] = jnp.where(low, turned, upper.reshape(256, 2 * HEAD_DIM)).reshape(
            32, 8, 2 * HEAD_DIM
        )

    @pl.loop(1, devices)
    def _(i):
        t = (lin + i) % devices
        remote(sb.at[t], rb.at[lin], b_send, b_recv, t // 4, t % 4).start()

    pltpu.make_async_copy(sb.at[lin], rb.at[lin], b_recv).start()

    slot_row = lax.broadcasted_iota(jnp.int32, (POOL, BLK), 0)
    wanted = [(t * POOL + slot_row).astype(F32) for t in (lin, own_tracks[0], own_tracks[1])]

    def add_counts(s, sums):
        codes = codes_of(s)
        return tuple(
            total + jnp.where(want == codes[0], 1.0, 0.0) + jnp.where(want == codes[1], 1.0, 0.0)
            for total, want in zip(sums, wanted)
        )

    zero = jnp.zeros((POOL, BLK), F32)
    counts = lax.fori_loop(0, n, add_counts, (zero, zero, zero))
    divisors = [jnp.maximum(jnp.sum(c, axis=1, keepdims=True), 1.0) for c in counts]

    drain(rb, b_recv)
    tiles = []
    for pair in range(8):
        sides = []
        for hd in (2 * pair, 2 * pair + 1):
            y, h = hd // 8, hd % 8
            side = None
            for c in range(2):
                for part in range(g):
                    piece = rb[(h * g + part) * 4 + 2 * y + c]
                    side = piece if side is None else side + piece
            sides.append(side)
        a, b = sides
        upper = jnp.where(low, pltpu.roll(a, HEAD_DIM, 1), b)
        lower = jnp.where(low, a, pltpu.roll(b, HEAD_DIM, 1))
        tiles.append((jnp.concatenate([upper, lower], axis=0) / divisors[0]).astype(BF))
    line = n // 2
    outer, inner = seq // 2, seq % 2
    sign = 1 - 2 * (outer // (line // 2))
    block = inner * 2 + yy
    mean = [jnp.concatenate(tiles[2 * k:2 * k + 2], axis=1) for k in range(4)]
    for k in range(4):
        m1[k, outer] = mean[k]

    def along(i):
        return (outer + sign * i + line) % line

    def plane(d):
        return (inner + d % 2) % 2, (yy + d // 2) % 2

    @pl.loop(1, line)
    def _(i):
        spot = m1.at[:, outer]
        remote(spot, spot, m_send, m_recv, along(i) * 2 + inner, head).start()

    for k in range(2):
        drain(wbuf.at[2 * yy + k], w_recv.at[2 * yy + k])
    drain(wbuf.at[2 * (1 - yy) + 1 - core], w_recv.at[2 * (1 - yy) + 1 - core])
    prediction = jnp.dot(mean[0], wbuf[0], preferred_element_type=F32)
    for k in range(1, 4):
        prediction += jnp.dot(mean[k], wbuf[k], preferred_element_type=F32)
    error_at = eb.at[core, block * line + outer]
    error_at[...] = (prediction - tgt_ref[head].astype(F32)).astype(BF)

    @pl.loop(1, line)
    def _(i):
        remote(
            error_at, error_at, e_send, e_recv.at[outer], along(i) * 2 + inner, head
        ).start()

    drain(m1.at[:, 0:line - 1], m_recv)
    mean_to = mb.at[core, pl.ds(block * line, line)]
    for d in range(4):
        to_inner, to_yy = plane(d)
        for c in range(2):
            to = 2 * to_yy + (core if c == 0 else 1 - core)
            if d == 0 and c == 0:
                pltpu.make_async_copy(m1.at[to], mean_to, m2_recv).start()
            else:
                remote(m1.at[to], mean_to, m2_send, m2_recv, outer * 2 + to_inner, to).start()

    @pl.loop(0, line)
    def _(i):
        spot = block * line + along(i)

        @pl.when(i > 0)
        def _():
            drain(eb.at[core, spot], e_recv.at[along(i)])

        for d in range(1, 4):
            to_inner, to_yy = plane(d)
            remote(
                eb.at[core, spot], eb.at[core, spot], e2_send, e2_recv.at[block],
                outer * 2 + to_inner, 2 * to_yy + core,
            ).start()

    for d in range(4):
        from_inner, from_yy = plane(d)
        other = from_inner * 2 + from_yy
        part = eb.at[core, pl.ds(other * line, line)]
        if d > 0:
            drain(part, e2_recv.at[other])
        remote(part, part, ef_send, ef_recv.at[other], seq, partner).start()

    drain(mb, m2_recv)

    own_code = jnp.concatenate(
        [(t * POOL + lax.broadcasted_iota(jnp.int32, (POOL, 1), 0)) for t in own_tracks], axis=0
    )
    picked = jnp.zeros((2 * POOL, w_ref.shape[1]), F32)
    for turn in range(2):
        side = core if turn == 0 else 1 - core
        if turn == 1:
            for o in range(4):
                drain(eb.at[side, pl.ds(o * line, line)], ef_recv.at[o])

        def gather(i, picked, side=side, fresh=turn == 0):
            means = mb[side, pl.ds(i * 16, 16)].reshape(256, -1)
            errors = eb[side, pl.ds(i * 16, 16)].reshape(256, -1)
            term = lax.dot_general(means, errors, TN, preferred_element_type=F32)
            if fresh:
                gacc[...] = term + jnp.where(i > 0, gacc[...], 0.0)
            else:
                gacc[...] += term
            spot = lax.broadcasted_iota(jnp.int32, (2 * POOL, 256), 1)
            where = i * 16 + spot // POOL
            track = 4 * (2 * (where % line) + where // (2 * line)) + 2 * (where // line % 2) + side
            code = track * POOL + spot % POOL
            pick = jnp.where(code == own_code, 1.0, 0.0).astype(BF)
            return picked + jnp.dot(pick, errors, preferred_element_type=F32)

        picked = lax.fori_loop(0, n // 8, gather, picked)

    greg_ref[...] = gacc[...].astype(BF)
    mean_grad = lax.dot_general(picked.astype(BF), w_ref[...], NT, preferred_element_type=F32)
    track_grad = (mean_grad / jnp.concatenate(divisors[1:], axis=0)).astype(BF)
    tgrad_ref[...] = track_grad

    first_sends(finish)
    drain(kvb.at[pl.ds(0, n // 2)], fw_send)
    w_across.wait_send()
    w_pair.wait_send()
    w_on.wait_send()
    drain(sb.at[pl.ds(0, devices - 1)], b_send)
    drain(m1.at[:, 0:line - 1], m_send)
    drain(eb.at[0, 0:7 * line // 4], m2_send)
    drain(eb.at[0, 0:line - 1], e_send)
    drain(eb.at[0, 0:3 * line], e2_send)
    drain(eb.at[0], ef_send)


def finish_kernel(part_ref, track_ref, rc_ref, ps_ref, greg_ref, cgrad_ref):
    greg_ref[...] = part_ref[...]
    lane_row = lax.broadcasted_iota(jnp.int32, (1, BLK), 1)
    slot_row = lax.broadcasted_iota(jnp.int32, (POOL, BLK), 0)
    for b in range(2):
        slot = jnp.where(lane_row < rc_ref[b], ps_ref[b:b + 1, :], -1)
        select = jnp.where(slot_row == slot, 1.0, 0.0).astype(BF)
        cgrad_ref[b * BLK:(b + 1) * BLK, :] = lax.dot_general(
            select, track_ref[b * POOL:(b + 1) * POOL], TN, preferred_element_type=F32
        ).astype(BF)


def solution(mesh):
    n = mesh.shape["seq"]
    devices = 4 * n

    def local(queries, keys, values, residual, weight, targets, block_track, row_count, slot):
        tok, width = queries.shape
        target_width = weight.shape[1]
        dma = pltpu.SemaphoreType.DMA
        vmem, smem = pl.BlockSpec(memory_space=pltpu.VMEM), pl.BlockSpec(memory_space=pltpu.SMEM)
        two = 2 * HEAD_DIM
        part, track_grad = pl.pallas_call(
            functools.partial(kernel, n),
            out_shape=(
                jax.ShapeDtypeStruct((width, target_width), BF),
                jax.ShapeDtypeStruct((2 * POOL, width), BF),
            ),
            in_specs=[vmem] * 6 + [smem, smem, vmem],
            out_specs=(vmem, vmem),
            scratch_shapes=[
                pltpu.VMEM((4, tok + INFO, two), BF),
                pltpu.VMEM((4, BLK, two), BF),
                pltpu.VMEM((4, BLK, two), BF),
                pltpu.VMEM((n, tok + INFO, two), BF),
                pltpu.VMEM((4, BLK, two), BF),
                pltpu.VMEM((4, BLK, two), BF),
                pltpu.VMEM((4 * tok, two), BF),
                pltpu.VMEM((4 * tok, two), BF),
                pltpu.VMEM((two, 2 * tok), BF),
                pltpu.VMEM((1, 4 * tok), F32),
                pltpu.VMEM((two, 4 * tok), F32),
                pltpu.VMEM((4, width, target_width), BF),
                pltpu.VMEM((devices, 8, two), F32),
                pltpu.VMEM((devices, 8, two), F32),
                pltpu.VMEM((4, n // 2, POOL, width), BF),
                pltpu.VMEM((2, 2 * n, POOL, width), BF),
                pltpu.VMEM((2, 2 * n, POOL, target_width), BF),
                pltpu.VMEM((width, target_width), F32),
                dma((4 * (n // 8),)),
                dma((n,)),
                dma((4,)),
                dma,
                dma((4,)),
                dma,
                dma,
                dma((3,)),
                dma((4,)),
                dma, dma, dma, dma, dma, dma,
                dma, dma((n // 2,)), dma, dma((4,)), dma, dma((4,)),
            ],
            compiler_params=pltpu.CompilerParams(
                collective_id=0, has_side_effects=True, vmem_limit_bytes=56 * 1024 * 1024
            ),
            cost_estimate=pl.CostEstimate(
                flops=4 * 4 * tok * n * tok * HEAD_DIM, bytes_accessed=8 * 1024 * 1024,
                transcendentals=4 * tok * n * tok,
            ),
        )(queries, keys, values, residual, weight, targets, block_track, row_count, slot)
        return pl.pallas_call(
            finish_kernel,
            out_shape=(
                jax.ShapeDtypeStruct((width, target_width), BF),
                jax.ShapeDtypeStruct((tok, width), BF),
            ),
            in_specs=[vmem, vmem, smem, vmem],
            out_specs=(vmem, vmem),
        )(part, track_grad, row_count, slot)

    return jax.shard_map(
        local,
        mesh=mesh,
        in_specs=(
            P("seq", "head"),
            P("seq", "head"),
            P("seq", "head"),
            P("seq", "head"),
            P("head", None),
            P("seq", None, None),
            P(),
            P("seq"),
            P("seq", None),
        ),
        out_specs=(P("head", None), P("seq", "head")),
        check_vma=False,
    )
```

```python
import functools

import jax
import jax.numpy as jnp
from jax import lax
from jax.experimental import pallas as pl
from jax.experimental.pallas import tpu as pltpu
from jax.sharding import PartitionSpec as P

HEAD_DIM = 64
BLK = 128
POOL = 16
INFO = 16
BF = jnp.bfloat16
F32 = jnp.float32
MESH = pl.DeviceIdType.MESH
NT = (((1,), (1,)), ((), ()))
TN = (((0,), (0,)), ((), ()))


def drain(ref, sem):
    pltpu.make_async_copy(ref, ref, sem).wait()


def remote(src, dst, send, recv, seq, head):
    return pltpu.make_async_remote_copy(
        src_ref=src, dst_ref=dst, send_sem=send, recv_sem=recv,
        device_id={"seq": seq, "head": head}, device_id_type=MESH,
    )


def kernel(
    n, q_ref, k_ref, v_ref, r_ref, w_ref, tgt_ref, bt_ref, rc_ref, ps_ref,
    greg_ref, tgrad_ref,
    kvs, qs, rs, kvb, qb, rb_in, qx, rx, vxt, run_max, acc, wbuf,
    row_code, row_weight, sums, parts, mb, tb, mean, picked, errors, gacc,
    kv_send, kv_recv, q_send, q_recv, r_send, r_recv, fw_send, w_send, w_recv, p_send, p_recv,
    m_send, m_recv, m2_send, m2_recv, m3_send, m3_recv,
    t_send, t_recv, t2_send, t2_recv, t3_send, t3_recv,
):
    g = n // 8
    blocks = 2 * n
    seq, head = lax.axis_index("seq"), lax.axis_index("head")
    core, yy = head % 2, head // 2
    partner, across = 2 * yy + 1 - core, (head + 2) % 4
    tok = q_ref.shape[0]
    line = n // 2
    outer, inner = seq // 2, seq % 2
    sign = 1 - 2 * (outer // (line // 2))
    block = inner * 2 + yy

    barrier = pltpu.get_barrier_semaphore()

    def greet(to_seq, to):
        pl.semaphore_signal(
            barrier, inc=1, device_id={"seq": to_seq, "head": to}, device_id_type=MESH
        )

    @pl.loop(1, 2 * n)
    def _(i):
        other = (seq * 2 + core + i) % (2 * n)
        greet(other // 2, 2 * yy + other % 2)

    for to_inner in range(2):
        greet(outer * 2 + to_inner, across)

    lane_row = lax.broadcasted_iota(jnp.int32, (1, BLK), 1)
    slots = [
        jnp.where(lane_row < rc_ref[b], ps_ref[b:b + 1, :], -1).astype(F32) for b in range(2)
    ]
    own_tracks = [bt_ref[2 * seq + b] for b in range(2)]
    row = lax.broadcasted_iota(jnp.int32, (INFO, BLK), 0)
    tracks = jnp.where(row == 2, own_tracks[0], own_tracks[1]).astype(F32)
    info = jnp.where(row == 0, slots[0], jnp.where(row == 1, slots[1], tracks)).astype(BF)
    for j in range(4):
        cols = slice(j * HEAD_DIM, (j + 1) * HEAD_DIM)
        qs[j] = jnp.concatenate([q_ref[0:BLK, cols], q_ref[BLK:, cols]], axis=1) * BF(HEAD_DIM ** -0.5)
        rs[j] = jnp.concatenate([r_ref[0:BLK, cols], r_ref[BLK:, cols]], axis=1)
        kvs[j, 0:tok, :] = jnp.concatenate([k_ref[:, cols], v_ref[:, cols]], axis=1)
        kvs[j, tok:tok + INFO, :] = info

    pl.semaphore_wait(barrier, 2 * n + 1)

    half, chunk = (seq // 4) % 2, seq // 8
    to_head = 2 * yy + half

    def first_sends(act):
        def whole(src, dst, send, recv):
            for j in range(4):
                lead = (4 * core + j) * g + chunk
                act(
                    jnp.logical_and(lead == seq, to_head == head),
                    remote(src.at[j], dst.at[seq % 4], send.at[j], recv, lead, to_head),
                    pltpu.make_async_copy(src.at[j], dst.at[seq % 4], recv),
                )

        whole(qs, qb, q_send, q_recv)
        for j in range(4):
            lead = (4 * core + j) * g
            for c in range(g):
                act(
                    jnp.logical_and(lead + c == seq, to_head == head),
                    remote(kvs.at[j], kvb.at[seq], kv_send.at[j * g + c], kv_recv.at[seq],
                           lead + c, to_head),
                    pltpu.make_async_copy(kvs.at[j], kvb.at[seq], kv_recv.at[seq]),
                )
        whole(rs, rb_in, r_send, r_recv)

    def begin(here, far, near):
        @pl.when(here)
        def _():
            near.start()

        @pl.when(jnp.logical_not(here))
        def _():
            far.start()

    def finish(here, far, near):
        @pl.when(jnp.logical_not(here))
        def _():
            far.wait_send()

    first_sends(begin)
    w_across = remote(w_ref, wbuf.at[head], w_send.at[0], w_recv.at[head], seq, across)
    w_pair = remote(w_ref, wbuf.at[head], w_send.at[1], w_recv.at[head], seq, partner)
    w_own = pltpu.make_async_copy(w_ref, wbuf.at[head], w_recv.at[head])
    w_across.start()
    w_pair.start()
    w_own.start()

    def along(i):
        return (outer + sign * i + line) % line

    def plane(d):
        return (inner + d % 2) % 2, (yy + d // 2) % 2

    def gather_along(buf, send, recv):
        own = buf.at[core, block * line + outer]

        @pl.loop(1, line)
        def _(i):
            remote(own, own, send, recv.at[outer], along(i) * 2 + inner, head).start()

    def gather_plane(buf, recv, send2, recv2):
        @pl.loop(0, line)
        def _(i):
            spot = buf.at[core, block * line + along(i)]

            @pl.when(i > 0)
            def _():
                drain(spot, recv.at[along(i)])

            for d in range(1, 4):
                to_inner, to_yy = plane(d)
                remote(
                    spot, spot, send2, recv2.at[block], outer * 2 + to_inner, 2 * to_yy + core
                ).start()

    def gather_pair(buf, recv2, send3, recv3):
        for d in range(4):
            from_inner, from_yy = plane(d)
            other = from_inner * 2 + from_yy
            spot = buf.at[core, pl.ds(other * line, line)]
            if d > 0:
                drain(spot, recv2.at[other])
            remote(spot, spot, send3, recv3.at[other], seq, partner).start()

    def gather_end(buf, recv3):
        for other in range(4):
            drain(buf.at[1 - core, pl.ds(other * line, line)], recv3.at[other])

    def gather_sent(buf, send, send2, send3):
        drain(buf.at[0, 0:line - 1], send)
        drain(buf.at[0, 0:3 * line], send2)
        drain(buf.at[0], send3)

    tb_own = tb.at[core, block * line + outer]
    tb_own[...] = tgt_ref[head]
    gather_along(tb, t_send, t_recv)

    slot_row = lax.broadcasted_iota(jnp.int32, (POOL, BLK), 0)

    def describe(b, earlier):
        track = bt_ref[b]
        row_code[b] = (track * POOL + slot_row).astype(F32)
        fresh = jnp.ones((POOL, BLK), F32)
        for other in earlier:
            fresh = jnp.where(slot_row * 0 + bt_ref[other] == track, 0.0, fresh)
        row_weight[b] = fresh

    for b in range(blocks):
        describe(b, range(b))

    run_max[...] = jnp.full_like(run_max, -1e30)
    acc[...] = jnp.zeros_like(acc)
    queries = qx.shape[0]
    low = lax.broadcasted_iota(jnp.int32, (1, 2 * HEAD_DIM), 1) < HEAD_DIM

    def unpack(src, dst, keep):
        for i in range(4):
            both = src[i].astype(F32)
            turned = pltpu.roll(both, HEAD_DIM, 1)
            first, second = (both, turned) if keep else (turned, both)
            mask = low if keep else jnp.logical_not(low)
            rest = 0.0 if keep else 1.0
            dst[2 * i * BLK:(2 * i + 1) * BLK, :] = jnp.where(mask, first, rest).astype(BF)
            dst[(2 * i + 1) * BLK:(2 * i + 2) * BLK, :] = jnp.where(mask, second, rest).astype(BF)

    drain(qb, q_recv)
    unpack(qb, qx, True)

    def attend(first):
        pair = kvb[pl.ds(first, 2), 0:tok, :].reshape(2 * tok, 2 * HEAD_DIM)
        vxt[...] = jnp.where(low, jnp.ones_like(pair), pair).T
        for t in range(queries // 256):
            cols = slice(t * 256, (t + 1) * 256)
            scores = lax.dot_general(pair, qx[cols, :], NT, preferred_element_type=F32)
            old = run_max[:, cols]
            new = jnp.maximum(old, jnp.max(scores, axis=0, keepdims=True))
            weights = jnp.exp(scores - new).astype(BF)
            acc[:, cols] = acc[:, cols] * jnp.exp(old - new) + jnp.dot(
                vxt[...], weights, preferred_element_type=F32
            )
            run_max[:, cols] = new

    @pl.loop(0, n // 4)
    def _(i):
        first = (i // 2) * 8 + 4 * core + 2 * (i % 2)
        for one in range(2):
            s = first + one
            drain(kvb.at[s], kv_recv.at[s])
            remote(kvb.at[s], kvb.at[s], fw_send, kv_recv.at[s], seq, partner).start()
        attend(first)

    drain(wbuf.at[across], w_recv.at[across])
    w_on = remote(wbuf.at[across], wbuf.at[across], w_send.at[2], w_recv.at[across], seq, partner)
    w_on.start()

    gather_plane(tb, t_recv, t2_send, t2_recv)

    @pl.loop(0, n // 4)
    def _(i):
        first = (i // 2) * 8 + 4 * (1 - core) + 2 * (i % 2)
        for one in range(2):
            drain(kvb.at[first + one], kv_recv.at[first + one])
        attend(first)

    def codes_of(s):
        lines = kvb[s, tok:tok + INFO, :].astype(F32)
        return [
            jnp.where(lines[b:b + 1] < 0, -1.0, POOL * lines[2 + b:3 + b] + lines[b:b + 1])
            for b in range(2)
        ]

    context = (acc[HEAD_DIM:, :] / acc[0:HEAD_DIM, :]).astype(BF)
    context = jnp.concatenate([jnp.zeros_like(context), context], axis=0)
    drain(rb_in, r_recv)
    unpack(rb_in, rx, False)

    here_first = (seq % g) * 8 + 4 * core
    here_codes = [code for i in range(4) for code in codes_of(here_first + i)]

    @pl.loop(0, n // 8)
    def _(i):
        code_rows = row_code[pl.ds(16 * i, 16)].reshape(256, BLK)
        pick = jnp.concatenate(
            [jnp.where(code_rows == code, 1.0, 0.0).astype(BF) for code in here_codes], axis=1
        )
        both = jnp.dot(pick, rx[...], preferred_element_type=F32) + lax.dot_general(
            pick, context, NT, preferred_element_type=F32
        )
        sums[pl.ds(2 * i, 2)] = both.reshape(2, BLK, 2 * HEAD_DIM)

    members = 2 * g
    lead = seq // g * g
    rank = seq % g * 2 + core

    for i in range(1, members):
        to = (rank + i) % members
        remote(
            sums.at[to], parts.at[members - 1 - i], p_send, p_recv, lead + to // 2, 2 * yy + to % 2
        ).start()

    gather_pair(tb, t2_recv, t3_send, t3_recv)
    drain(parts.at[0:members - 1], p_recv)
    whole_sum = sums[rank]
    for i in range(members - 1):
        whole_sum = whole_sum + parts[i]
    turned = pltpu.roll(whole_sum, HEAD_DIM, 1)
    wide = jnp.where(low, whole_sum, turned)
    own_mean = jnp.where(low, turned, whole_sum) / jnp.maximum(wide, 1.0)
    half_rows = BLK // 2
    mb_own = mb.at[core, block * line + outer]
    mb_own[...] = jnp.where(
        low, own_mean[half_rows:], own_mean[0:half_rows]
    ).astype(BF)
    gather_along(mb, m_send, m_recv)

    gather_end(tb, t3_recv)

    @pl.loop(0, n // 8)
    def _(i):
        code_rows = row_code[pl.ds(16 * i, 16)].reshape(256, BLK)[:, 0:1]
        spot = lax.broadcasted_iota(jnp.int32, (256, 32 * n), 1)
        place = spot // POOL
        found = None
        for side in (core, 1 - core):
            track = 4 * (2 * (place % line) + place // (2 * line)) + 2 * (place // line % 2) + side
            code = (track * POOL + spot % POOL).astype(F32)
            pick = jnp.where(code == code_rows, 1.0, 0.0).astype(BF)
            term = jnp.dot(pick, tb[side].reshape(32 * n, -1), preferred_element_type=F32)
            found = term if found is None else found + term
        picked[i] = found.astype(BF)

    wanted = [(t * POOL + slot_row).astype(F32) for t in own_tracks]

    def add_counts(s, totals):
        codes = codes_of(s)
        return tuple(
            total + jnp.where(want == codes[0], 1.0, 0.0) + jnp.where(want == codes[1], 1.0, 0.0)
            for total, want in zip(totals, wanted)
        )

    zero = jnp.zeros((POOL, BLK), F32)
    counts = lax.fori_loop(0, n, add_counts, (zero, zero))
    divisors = [jnp.maximum(jnp.sum(c, axis=1, keepdims=True), 1.0) for c in counts]
    for k in range(2):
        drain(wbuf.at[2 * yy + k], w_recv.at[2 * yy + k])
    drain(wbuf.at[2 * (1 - yy) + 1 - core], w_recv.at[2 * (1 - yy) + 1 - core])

    gather_plane(mb, m_recv, m2_send, m2_recv)
    gather_pair(mb, m2_recv, m3_send, m3_recv)
    gather_end(mb, m3_recv)

    for part in range(members):
        side, share = (core if part % 2 == 0 else 1 - core), part // 2
        for pair in range(8):
            two = []
            for hd in (2 * pair, 2 * pair + 1):
                y, s = hd // 8, hd % 8 * g + share
                two.append(mb[side, (s % 2 * 2 + y) * line + s // 2].astype(F32))
            a, b = two
            at = slice(pair % 2 * BLK, pair % 2 * BLK + BLK)
            mean[pair // 2, share, side, 0:half_rows, at] = jnp.where(
                low, pltpu.roll(a, HEAD_DIM, 1), b
            ).astype(BF)
            mean[pair // 2, share, side, half_rows:BLK, at] = jnp.where(
                low, a, pltpu.roll(b, HEAD_DIM, 1)
            ).astype(BF)

    @pl.loop(0, n // 8)
    def _(i):
        prediction = jnp.dot(mean[0, i].reshape(256, -1), wbuf[0], preferred_element_type=F32)
        for k in range(1, 4):
            prediction += jnp.dot(mean[k, i].reshape(256, -1), wbuf[k], preferred_element_type=F32)
        error = (prediction - picked[i].astype(F32)).astype(BF)
        errors[pl.ds(8 * i, 8)] = error.reshape(8, 2 * POOL, -1)
        weight = row_weight[pl.ds(16 * i, 16)].reshape(256, BLK)[:, 0:1]
        once = (mean[head, i].reshape(256, -1).astype(F32) * weight).astype(BF)
        term = lax.dot_general(once, error, TN, preferred_element_type=F32)
        gacc[...] = term + jnp.where(i > 0, gacc[...], 0.0)

    greg_ref[...] = gacc[...].astype(BF)
    mean_grad = lax.dot_general(errors[seq], w_ref[...], NT, preferred_element_type=F32)
    tgrad_ref[...] = (mean_grad / jnp.concatenate(divisors, axis=0)).astype(BF)

    first_sends(finish)
    drain(kvb.at[pl.ds(0, n // 2)], fw_send)
    w_across.wait_send()
    w_pair.wait_send()
    w_on.wait_send()
    drain(sums.at[pl.ds(0, members - 1)], p_send)
    gather_sent(mb, m_send, m2_send, m3_send)
    gather_sent(tb, t_send, t2_send, t3_send)


def finish_kernel(part_ref, track_ref, rc_ref, ps_ref, greg_ref, cgrad_ref):
    greg_ref[...] = part_ref[...]
    lane_row = lax.broadcasted_iota(jnp.int32, (1, BLK), 1)
    slot_row = lax.broadcasted_iota(jnp.int32, (POOL, BLK), 0)
    for b in range(2):
        slot = jnp.where(lane_row < rc_ref[b], ps_ref[b:b + 1, :], -1)
        select = jnp.where(slot_row == slot, 1.0, 0.0).astype(BF)
        cgrad_ref[b * BLK:(b + 1) * BLK, :] = lax.dot_general(
            select, track_ref[b * POOL:(b + 1) * POOL], TN, preferred_element_type=F32
        ).astype(BF)


def solution(mesh):
    n = mesh.shape["seq"]
    members = n // 4

    def local(queries, keys, values, residual, weight, targets, block_track, row_count, slot):
        tok, width = queries.shape
        target_width = weight.shape[1]
        dma = pltpu.SemaphoreType.DMA
        vmem, smem = pl.BlockSpec(memory_space=pltpu.VMEM), pl.BlockSpec(memory_space=pltpu.SMEM)
        two = 2 * HEAD_DIM
        part, track_grad = pl.pallas_call(
            functools.partial(kernel, n),
            out_shape=(
                jax.ShapeDtypeStruct((width, target_width), BF),
                jax.ShapeDtypeStruct((2 * POOL, width), BF),
            ),
            in_specs=[vmem] * 6 + [smem, smem, vmem],
            out_specs=(vmem, vmem),
            scratch_shapes=[
                pltpu.VMEM((4, tok + INFO, two), BF),
                pltpu.VMEM((4, BLK, two), BF),
                pltpu.VMEM((4, BLK, two), BF),
                pltpu.VMEM((n, tok + INFO, two), BF),
                pltpu.VMEM((4, BLK, two), BF),
                pltpu.VMEM((4, BLK, two), BF),
                pltpu.VMEM((4 * tok, two), BF),
                pltpu.VMEM((4 * tok, two), BF),
                pltpu.VMEM((two, 2 * tok), BF),
                pltpu.VMEM((1, 4 * tok), F32),
                pltpu.VMEM((two, 4 * tok), F32),
                pltpu.VMEM((4, width, target_width), BF),
                pltpu.VMEM((2 * n, POOL, BLK), F32),
                pltpu.VMEM((2 * n, POOL, BLK), F32),
                pltpu.VMEM((members, BLK, two), F32),
                pltpu.VMEM((members - 1, BLK, two), F32),
                pltpu.VMEM((2, 2 * n, BLK // 2, two), BF),
                pltpu.VMEM((2, 2 * n, POOL, target_width), BF),
                pltpu.VMEM((4, n // 8, 2, BLK, width), BF),
                pltpu.VMEM((n // 8, 256, target_width), BF),
                pltpu.VMEM((n, 2 * POOL, target_width), BF),
                pltpu.VMEM((width, target_width), F32),
                dma((4 * (n // 8),)),
                dma((n,)),
                dma((4,)),
                dma,
                dma((4,)),
                dma,
                dma,
                dma((3,)),
                dma((4,)),
                dma, dma,
                dma, dma((n // 2,)), dma, dma((4,)), dma, dma((4,)),
                dma, dma((n // 2,)), dma, dma((4,)), dma, dma((4,)),
            ],
            compiler_params=pltpu.CompilerParams(
                collective_id=0, has_side_effects=True, vmem_limit_bytes=56 * 1024 * 1024
            ),
            cost_estimate=pl.CostEstimate(
                flops=4 * 4 * tok * n * tok * HEAD_DIM, bytes_accessed=8 * 1024 * 1024,
                transcendentals=4 * tok * n * tok,
            ),
        )(queries, keys, values, residual, weight, targets, block_track, row_count, slot)
        return pl.pallas_call(
            finish_kernel,
            out_shape=(
                jax.ShapeDtypeStruct((width, target_width), BF),
                jax.ShapeDtypeStruct((tok, width), BF),
            ),
            in_specs=[vmem, vmem, smem, vmem],
            out_specs=(vmem, vmem),
        )(part, track_grad, row_count, slot)

    return jax.shard_map(
        local,
        mesh=mesh,
        in_specs=(
            P("seq", "head"),
            P("seq", "head"),
            P("seq", "head"),
            P("seq", "head"),
            P("head", None),
            P("seq", None, None),
            P(),
            P("seq"),
            P("seq", None),
        ),
        out_specs=(P("head", None), P("seq", "head")),
        check_vma=False,
    )
```

```python
import functools

import jax
import jax.numpy as jnp
from jax import lax
from jax.experimental import pallas as pl
from jax.experimental.pallas import tpu as pltpu
from jax.sharding import PartitionSpec as P

HEAD_DIM = 64
BLK = 128
POOL = 16
INFO = 16
BF = jnp.bfloat16
F32 = jnp.float32
MESH = pl.DeviceIdType.MESH
NT = (((1,), (1,)), ((), ()))
TN = (((0,), (0,)), ((), ()))


def drain(ref, sem):
    pltpu.make_async_copy(ref, ref, sem).wait()


def remote(src, dst, send, recv, seq, head):
    return pltpu.make_async_remote_copy(
        src_ref=src, dst_ref=dst, send_sem=send, recv_sem=recv,
        device_id={"seq": seq, "head": head}, device_id_type=MESH,
    )


def kernel(
    n, q_ref, k_ref, v_ref, r_ref, w_ref, tgt_ref, bt_ref, rc_ref, ps_ref,
    greg_ref, tgrad_ref,
    kvs, qs, rs, kvb, qb, rb_in, qx, rx, vxt, run_max, acc, wbuf,
    row_code, row_weight, sums, parts, mb, tb, mean, picked, errors, gacc,
    kv_send, kv_recv, q_send, q_recv, r_send, r_recv, fw_send, w_send, w_recv, p_send, p_recv,
    m_send, m_recv, m2_send, m2_recv, m3_send, m3_recv,
    t_send, t_recv, t2_send, t2_recv, t3_send, t3_recv,
):
    g = n // 8
    blocks = 2 * n
    seq, head = lax.axis_index("seq"), lax.axis_index("head")
    core, yy = head % 2, head // 2
    partner, across = 2 * yy + 1 - core, (head + 2) % 4
    tok = q_ref.shape[0]
    line = n // 2
    outer, inner = seq // 2, seq % 2
    sign = 1 - 2 * (outer // (line // 2))
    block = inner * 2 + yy

    barrier = pltpu.get_barrier_semaphore()

    def greet(to_seq, to):
        pl.semaphore_signal(
            barrier, inc=1, device_id={"seq": to_seq, "head": to}, device_id_type=MESH
        )

    @pl.loop(1, 2 * n)
    def _(i):
        other = (seq * 2 + core + i) % (2 * n)
        greet(other // 2, 2 * yy + other % 2)

    for to_inner in range(2):
        greet(outer * 2 + to_inner, across)

    lane_row = lax.broadcasted_iota(jnp.int32, (1, BLK), 1)
    slots = [
        jnp.where(lane_row < rc_ref[b], ps_ref[b:b + 1, :], -1).astype(F32) for b in range(2)
    ]
    own_tracks = [bt_ref[2 * seq + b] for b in range(2)]
    row = lax.broadcasted_iota(jnp.int32, (INFO, BLK), 0)
    tracks = jnp.where(row == 2, own_tracks[0], own_tracks[1]).astype(F32)
    info = jnp.where(row == 0, slots[0], jnp.where(row == 1, slots[1], tracks)).astype(BF)
    for j in range(4):
        cols = slice(j * HEAD_DIM, (j + 1) * HEAD_DIM)
        qs[j] = jnp.concatenate([q_ref[0:BLK, cols], q_ref[BLK:, cols]], axis=1) * BF(HEAD_DIM ** -0.5)
        rs[j] = jnp.concatenate([r_ref[0:BLK, cols], r_ref[BLK:, cols]], axis=1)
        kvs[j, 0:tok, :] = jnp.concatenate([k_ref[:, cols], v_ref[:, cols]], axis=1)
        kvs[j, tok:tok + INFO, :] = info

    pl.semaphore_wait(barrier, 2 * n + 1)

    half, chunk = (seq // 4) % 2, seq // 8
    to_head = 2 * yy + half

    def first_sends(act):
        def whole(src, dst, send, recv):
            for j in range(4):
                lead = (4 * core + j) * g + chunk
                act(
                    jnp.logical_and(lead == seq, to_head == head),
                    remote(src.at[j], dst.at[seq % 4], send.at[j], recv, lead, to_head),
                    pltpu.make_async_copy(src.at[j], dst.at[seq % 4], recv),
                )

        whole(qs, qb, q_send, q_recv)
        for j in range(4):
            lead = (4 * core + j) * g
            for c in range(g):
                act(
                    jnp.logical_and(lead + c == seq, to_head == head),
                    remote(kvs.at[j], kvb.at[seq], kv_send.at[j * g + c], kv_recv.at[seq],
                           lead + c, to_head),
                    pltpu.make_async_copy(kvs.at[j], kvb.at[seq], kv_recv.at[seq]),
                )
        whole(rs, rb_in, r_send, r_recv)

    def begin(here, far, near):
        @pl.when(here)
        def _():
            near.start()

        @pl.when(jnp.logical_not(here))
        def _():
            far.start()

    def finish(here, far, near):
        @pl.when(jnp.logical_not(here))
        def _():
            far.wait_send()

    first_sends(begin)
    w_across = remote(w_ref, wbuf.at[head], w_send.at[0], w_recv.at[head], seq, across)
    w_pair = remote(w_ref, wbuf.at[head], w_send.at[1], w_recv.at[head], seq, partner)
    w_own = pltpu.make_async_copy(w_ref, wbuf.at[head], w_recv.at[head])
    w_across.start()
    w_pair.start()
    w_own.start()

    def along(i):
        return (outer + sign * i + line) % line

    def plane(d):
        return (inner + d % 2) % 2, (yy + d // 2) % 2

    def gather_along(buf, send, recv):
        own = buf.at[core, block * line + outer]

        @pl.loop(1, line)
        def _(i):
            remote(own, own, send, recv.at[outer], along(i) * 2 + inner, head).start()

    def gather_plane(buf, recv, send2, recv2):
        @pl.loop(0, line)
        def _(i):
            spot = buf.at[core, block * line + along(i)]

            @pl.when(i > 0)
            def _():
                drain(spot, recv.at[along(i)])

            for d in range(1, 4):
                to_inner, to_yy = plane(d)
                remote(
                    spot, spot, send2, recv2.at[block], outer * 2 + to_inner, 2 * to_yy + core
                ).start()

    def gather_pair(buf, recv2, send3, recv3):
        for d in range(4):
            from_inner, from_yy = plane(d)
            other = from_inner * 2 + from_yy
            spot = buf.at[core, pl.ds(other * line, line)]
            if d > 0:
                drain(spot, recv2.at[other])
            remote(spot, spot, send3, recv3.at[other], seq, partner).start()

    def gather_end(buf, recv3):
        for other in range(4):
            drain(buf.at[1 - core, pl.ds(other * line, line)], recv3.at[other])

    def gather_sent(buf, send, send2, send3):
        drain(buf.at[0, 0:line - 1], send)
        drain(buf.at[0, 0:3 * line], send2)
        drain(buf.at[0], send3)

    tb_own = tb.at[core, block * line + outer]
    tb_own[...] = tgt_ref[head]
    gather_along(tb, t_send, t_recv)

    slot_row = lax.broadcasted_iota(jnp.int32, (POOL, BLK), 0)

    def describe(b, earlier):
        track = bt_ref[b]
        row_code[b] = (track * POOL + slot_row).astype(F32)
        fresh = jnp.ones((POOL, BLK), F32)
        for other in earlier:
            fresh = jnp.where(slot_row * 0 + bt_ref[other] == track, 0.0, fresh)
        row_weight[b] = fresh

    for b in range(blocks):
        describe(b, range(b))

    run_max[...] = jnp.full_like(run_max, -1e30)
    acc[...] = jnp.zeros_like(acc)
    queries = qx.shape[0]
    low = lax.broadcasted_iota(jnp.int32, (1, 2 * HEAD_DIM), 1) < HEAD_DIM

    def unpack(src, dst, keep):
        for i in range(4):
            both = src[i].astype(F32)
            turned = pltpu.roll(both, HEAD_DIM, 1)
            first, second = (both, turned) if keep else (turned, both)
            mask = low if keep else jnp.logical_not(low)
            rest = 0.0 if keep else 1.0
            dst[2 * i * BLK:(2 * i + 1) * BLK, :] = jnp.where(mask, first, rest).astype(BF)
            dst[(2 * i + 1) * BLK:(2 * i + 2) * BLK, :] = jnp.where(mask, second, rest).astype(BF)

    drain(qb, q_recv)
    unpack(qb, qx, True)

    def attend(first):
        pair = kvb[pl.ds(first, 2), 0:tok, :].reshape(2 * tok, 2 * HEAD_DIM)
        vxt[...] = jnp.where(low, jnp.ones_like(pair), pair).T
        for t in range(queries // 256):
            cols = slice(t * 256, (t + 1) * 256)
            scores = lax.dot_general(pair, qx[cols, :], NT, preferred_element_type=F32)
            old = run_max[:, cols]
            new = jnp.maximum(old, jnp.max(scores, axis=0, keepdims=True))
            weights = jnp.exp(scores - new).astype(BF)
            acc[:, cols] = acc[:, cols] * jnp.exp(old - new) + jnp.dot(
                vxt[...], weights, preferred_element_type=F32
            )
            run_max[:, cols] = new

    @pl.loop(0, n // 4)
    def _(i):
        first = (i // 2) * 8 + 4 * core + 2 * (i % 2)
        for one in range(2):
            s = first + one
            drain(kvb.at[s], kv_recv.at[s])
            remote(kvb.at[s], kvb.at[s], fw_send, kv_recv.at[s], seq, partner).start()
        attend(first)

    drain(wbuf.at[across], w_recv.at[across])
    w_on = remote(wbuf.at[across], wbuf.at[across], w_send.at[2], w_recv.at[across], seq, partner)
    w_on.start()

    gather_plane(tb, t_recv, t2_send, t2_recv)

    @pl.loop(0, n // 4)
    def _(i):
        first = (i // 2) * 8 + 4 * (1 - core) + 2 * (i % 2)
        for one in range(2):
            drain(kvb.at[first + one], kv_recv.at[first + one])
        attend(first)

    def codes_of(s):
        lines = kvb[s, tok:tok + INFO, :].astype(F32)
        return [
            jnp.where(lines[b:b + 1] < 0, -1.0, POOL * lines[2 + b:3 + b] + lines[b:b + 1])
            for b in range(2)
        ]

    context = (acc[HEAD_DIM:, :] / acc[0:HEAD_DIM, :]).astype(BF)
    context = jnp.concatenate([jnp.zeros_like(context), context], axis=0)
    drain(rb_in, r_recv)
    unpack(rb_in, rx, False)

    here_first = (seq % g) * 8 + 4 * core
    here_codes = [code for i in range(4) for code in codes_of(here_first + i)]

    @pl.loop(0, n // 8)
    def _(i):
        code_rows = row_code[pl.ds(16 * i, 16)].reshape(256, BLK)
        pick = jnp.concatenate(
            [jnp.where(code_rows == code, 1.0, 0.0).astype(BF) for code in here_codes], axis=1
        )
        both = jnp.dot(pick, rx[...], preferred_element_type=F32) + lax.dot_general(
            pick, context, NT, preferred_element_type=F32
        )
        sums[pl.ds(2 * i, 2)] = both.reshape(2, BLK, 2 * HEAD_DIM)

    members = 2 * g
    lead = seq // g * g
    rank = seq % g * 2 + core

    for i in range(1, members):
        to = (rank + i) % members
        remote(
            sums.at[to], parts.at[members - 1 - i], p_send, p_recv, lead + to // 2, 2 * yy + to % 2
        ).start()

    gather_pair(tb, t2_recv, t3_send, t3_recv)
    drain(parts.at[0:members - 1], p_recv)
    whole_sum = sums[rank]
    for i in range(members - 1):
        whole_sum = whole_sum + parts[i]
    turned = pltpu.roll(whole_sum, HEAD_DIM, 1)
    wide = jnp.where(low, whole_sum, turned)
    own_mean = jnp.where(low, turned, whole_sum) / jnp.maximum(wide, 1.0)
    half_rows = BLK // 2
    mb_own = mb.at[core, block * line + outer]
    mb_own[...] = jnp.where(
        low, own_mean[half_rows:], own_mean[0:half_rows]
    ).astype(BF)
    gather_along(mb, m_send, m_recv)

    wanted = [(t * POOL + slot_row).astype(F32) for t in own_tracks]

    def add_counts(s, totals):
        codes = codes_of(s)
        return tuple(
            total + jnp.where(want == codes[0], 1.0, 0.0) + jnp.where(want == codes[1], 1.0, 0.0)
            for total, want in zip(totals, wanted)
        )

    zero = jnp.zeros((POOL, BLK), F32)
    counts = lax.fori_loop(0, n, add_counts, (zero, zero))
    divisors = [jnp.maximum(jnp.sum(c, axis=1, keepdims=True), 1.0) for c in counts]
    for k in range(2):
        drain(wbuf.at[2 * yy + k], w_recv.at[2 * yy + k])
    drain(wbuf.at[2 * (1 - yy) + 1 - core], w_recv.at[2 * (1 - yy) + 1 - core])

    gather_plane(mb, m_recv, m2_send, m2_recv)

    gather_end(tb, t3_recv)

    @pl.loop(0, n // 8)
    def _(i):
        code_rows = row_code[pl.ds(16 * i, 16)].reshape(256, BLK)[:, 0:1]
        spot = lax.broadcasted_iota(jnp.int32, (256, 32 * n), 1)
        place = spot // POOL
        found = None
        for side in (core, 1 - core):
            track = 4 * (2 * (place % line) + place // (2 * line)) + 2 * (place // line % 2) + side
            code = (track * POOL + spot % POOL).astype(F32)
            pick = jnp.where(code == code_rows, 1.0, 0.0).astype(BF)
            term = jnp.dot(pick, tb[side].reshape(32 * n, -1), preferred_element_type=F32)
            found = term if found is None else found + term
        picked[i] = found.astype(BF)

    gather_pair(mb, m2_recv, m3_send, m3_recv)
    gather_end(mb, m3_recv)

    for part in range(members):
        side, share = (core if part % 2 == 0 else 1 - core), part // 2
        for pair in range(8):
            two = []
            for hd in (2 * pair, 2 * pair + 1):
                y, s = hd // 8, hd % 8 * g + share
                two.append(mb[side, (s % 2 * 2 + y) * line + s // 2].astype(F32))
            a, b = two
            at = slice(pair % 2 * BLK, pair % 2 * BLK + BLK)
            mean[pair // 2, share, side, 0:half_rows, at] = jnp.where(
                low, pltpu.roll(a, HEAD_DIM, 1), b
            ).astype(BF)
            mean[pair // 2, share, side, half_rows:BLK, at] = jnp.where(
                low, a, pltpu.roll(b, HEAD_DIM, 1)
            ).astype(BF)

    @pl.loop(0, n // 8)
    def _(i):
        prediction = jnp.dot(mean[0, i].reshape(256, -1), wbuf[0], preferred_element_type=F32)
        for k in range(1, 4):
            prediction += jnp.dot(mean[k, i].reshape(256, -1), wbuf[k], preferred_element_type=F32)
        error = (prediction - picked[i].astype(F32)).astype(BF)
        errors[pl.ds(8 * i, 8)] = error.reshape(8, 2 * POOL, -1)
        weight = row_weight[pl.ds(16 * i, 16)].reshape(256, BLK)[:, 0:1]
        once = (mean[head, i].reshape(256, -1).astype(F32) * weight).astype(BF)
        term = lax.dot_general(once, error, TN, preferred_element_type=F32)
        gacc[...] = term + jnp.where(i > 0, gacc[...], 0.0)

    greg_ref[...] = gacc[...].astype(BF)
    mean_grad = lax.dot_general(errors[seq], w_ref[...], NT, preferred_element_type=F32)
    tgrad_ref[...] = (mean_grad / jnp.concatenate(divisors, axis=0)).astype(BF)

    first_sends(finish)
    drain(kvb.at[pl.ds(0, n // 2)], fw_send)
    w_across.wait_send()
    w_pair.wait_send()
    w_on.wait_send()
    drain(sums.at[pl.ds(0, members - 1)], p_send)
    gather_sent(mb, m_send, m2_send, m3_send)
    gather_sent(tb, t_send, t2_send, t3_send)


def finish_kernel(part_ref, track_ref, rc_ref, ps_ref, greg_ref, cgrad_ref):
    greg_ref[...] = part_ref[...]
    lane_row = lax.broadcasted_iota(jnp.int32, (1, BLK), 1)
    slot_row = lax.broadcasted_iota(jnp.int32, (POOL, BLK), 0)
    for b in range(2):
        slot = jnp.where(lane_row < rc_ref[b], ps_ref[b:b + 1, :], -1)
        select = jnp.where(slot_row == slot, 1.0, 0.0).astype(BF)
        cgrad_ref[b * BLK:(b + 1) * BLK, :] = lax.dot_general(
            select, track_ref[b * POOL:(b + 1) * POOL], TN, preferred_element_type=F32
        ).astype(BF)


def solution(mesh):
    n = mesh.shape["seq"]
    members = n // 4

    def local(queries, keys, values, residual, weight, targets, block_track, row_count, slot):
        tok, width = queries.shape
        target_width = weight.shape[1]
        dma = pltpu.SemaphoreType.DMA
        vmem, smem = pl.BlockSpec(memory_space=pltpu.VMEM), pl.BlockSpec(memory_space=pltpu.SMEM)
        two = 2 * HEAD_DIM
        part, track_grad = pl.pallas_call(
            functools.partial(kernel, n),
            out_shape=(
                jax.ShapeDtypeStruct((width, target_width), BF),
                jax.ShapeDtypeStruct((2 * POOL, width), BF),
            ),
            in_specs=[vmem] * 6 + [smem, smem, vmem],
            out_specs=(vmem, vmem),
            scratch_shapes=[
                pltpu.VMEM((4, tok + INFO, two), BF),
                pltpu.VMEM((4, BLK, two), BF),
                pltpu.VMEM((4, BLK, two), BF),
                pltpu.VMEM((n, tok + INFO, two), BF),
                pltpu.VMEM((4, BLK, two), BF),
                pltpu.VMEM((4, BLK, two), BF),
                pltpu.VMEM((4 * tok, two), BF),
                pltpu.VMEM((4 * tok, two), BF),
                pltpu.VMEM((two, 2 * tok), BF),
                pltpu.VMEM((1, 4 * tok), F32),
                pltpu.VMEM((two, 4 * tok), F32),
                pltpu.VMEM((4, width, target_width), BF),
                pltpu.VMEM((2 * n, POOL, BLK), F32),
                pltpu.VMEM((2 * n, POOL, BLK), F32),
                pltpu.VMEM((members, BLK, two), F32),
                pltpu.VMEM((members - 1, BLK, two), F32),
                pltpu.VMEM((2, 2 * n, BLK // 2, two), BF),
                pltpu.VMEM((2, 2 * n, POOL, target_width), BF),
                pltpu.VMEM((4, n // 8, 2, BLK, width), BF),
                pltpu.VMEM((n // 8, 256, target_width), BF),
                pltpu.VMEM((n, 2 * POOL, target_width), BF),
                pltpu.VMEM((width, target_width), F32),
                dma((4 * (n // 8),)),
                dma((n,)),
                dma((4,)),
                dma,
                dma((4,)),
                dma,
                dma,
                dma((3,)),
                dma((4,)),
                dma, dma,
                dma, dma((n // 2,)), dma, dma((4,)), dma, dma((4,)),
                dma, dma((n // 2,)), dma, dma((4,)), dma, dma((4,)),
            ],
            compiler_params=pltpu.CompilerParams(
                collective_id=0, has_side_effects=True, vmem_limit_bytes=56 * 1024 * 1024
            ),
            cost_estimate=pl.CostEstimate(
                flops=4 * 4 * tok * n * tok * HEAD_DIM, bytes_accessed=8 * 1024 * 1024,
                transcendentals=4 * tok * n * tok,
            ),
        )(queries, keys, values, residual, weight, targets, block_track, row_count, slot)
        return pl.pallas_call(
            finish_kernel,
            out_shape=(
                jax.ShapeDtypeStruct((width, target_width), BF),
                jax.ShapeDtypeStruct((tok, width), BF),
            ),
            in_specs=[vmem, vmem, smem, vmem],
            out_specs=(vmem, vmem),
        )(part, track_grad, row_count, slot)

    return jax.shard_map(
        local,
        mesh=mesh,
        in_specs=(
            P("seq", "head"),
            P("seq", "head"),
            P("seq", "head"),
            P("seq", "head"),
            P("head", None),
            P("seq", None, None),
            P(),
            P("seq"),
            P("seq", None),
        ),
        out_specs=(P("head", None), P("seq", "head")),
        check_vma=False,
    )
```
